32 devices in a mesh: brick: 4 (over y, x), section: 2 (over core), dp: 4 (over z).
Axes of the slice: x: 2, y: 2, z: 4, core: 2. Of those that a mesh axis runs over, the one named last changes fastest.
Arguments:
- features: bfloat16 [2, 4, 16, 512, 128], P('section', 'dp', 'brick'), may hold values from -6 to 6
- weights: bfloat16 [2, 27, 128, 128], P('section'), may hold values from -0.109375 to 0.109375
- projection: bfloat16 [128, 128], replicated, may hold values from -0.5 to 0.5
- cotangent: bfloat16 [2, 4, 16, 512, 128], P('section', 'dp', 'brick'), may hold values from -0.078125 to 0.078125
- neighbours: int32 [2, 4, 16, 6], P('section', 'dp', 'brick'), may hold values from -1 to 15, as said below
- route: int32 [4, 16], P('dp', 'brick'), may hold values from 0 to 15, as said below
Outputs:
- activations: bfloat16 [2, 4, 16, 512, 128], P('section', 'dp', 'brick')
- weight_grads: float32 [2, 27, 128, 128], P('section')
- projection_grad: float32 [128, 128], replicated
The draws below stay inside these ranges and needn't reach their ends.
Inputs may be any that keep to these rules, and one draw needn't show every extreme that they name: `neighbours`: owners hold 4 consecutive rows each. Entries 2 to 5 name bricks of the same owner; entry 0 names a brick of the same or the next owner, entry 1 of the same or the previous owner. `route`: each scene's row is a permutation of its bricks; every decoder owner receives 4 bricks; the bricks of one encoder owner go to at most 2 rows of one decoder owner, and every encoder owner sends exactly 2 to some decoder owner.
All inputs are finite; a program needn't handle non-finite values.
Results may differ from the reference program's by a relative error of at most 0.0059.
Values may be sent and summed in bfloat16 or wider, within the bound.
A program may use at most 128 MiB of HBM per device.

```python
import jax
import jax.numpy as jnp
from jax import lax

C = 128
BR = 4
SCENES = 4
BRICKS = 16


def draw_neighbours(key, part):
    key = jax.random.fold_in(key, 5)
    keys = jax.random.split(key, 8)
    shape = (2, SCENES, BRICKS)
    rows = jnp.arange(BRICKS, dtype=jnp.int32)
    owner = rows // BR
    owners = BRICKS // BR
    base = (owner * BR)[None, None, :]
    cross_up = (jax.random.randint(keys[0], shape, 0, 2) == 1) & (owner < owners - 1)[None, None, :]
    far_up = base + BR + jax.random.randint(keys[1], shape, 0, BR)
    entry_up = jnp.where(cross_up, far_up, base + jax.random.randint(keys[2], shape, 0, BR))
    cross_down = (jax.random.randint(keys[3], shape, 0, 2) == 1) & (owner > 0)[None, None, :]
    far_down = base - BR + jax.random.randint(keys[4], shape, 0, BR)
    entry_down = jnp.where(cross_down, far_down, base + jax.random.randint(keys[5], shape, 0, BR))
    others = base[..., None] + jax.random.randint(keys[6], shape + (4,), 0, BR)
    values = jnp.concatenate([entry_up[..., None], entry_down[..., None], others], -1)
    keeping = jax.random.randint(keys[7], shape + (6,), 0, 5) > 0
    values = jnp.where(keeping, values, -1)
    values = values.at[:, :, 0, 1].set(-1)
    values = values.at[:, :, BRICKS - 2, 2].set(BRICKS - 1)
    return values.astype(jnp.int32)


def draw_route(key, part):
    key = jax.random.fold_in(key, 9)
    owners = BRICKS // BR
    capacity = max(2, 3 * BR // (2 * owners))
    cycle = max(owners - 1, 1)

    def one_scene(scene_key):
        keys = jax.random.split(scene_key, 5)
        perm_in = jax.random.permutation(keys[0], owners)
        perm_out = jax.random.permutation(keys[1], owners)
        offset_start = jax.random.randint(keys[2], (), 0, cycle)
        groups = jnp.arange(BR, dtype=jnp.int32)
        shifted = jnp.where(groups < capacity, 0, 1 + (groups - capacity + offset_start) % cycle)
        order = jax.vmap(lambda inner: jax.random.permutation(inner, BR))(jax.random.split(keys[3], owners))
        target = perm_out[(perm_in[:, None] + shifted[order]) % owners]
        offsets = jax.vmap(lambda inner: jax.random.permutation(inner, BR))(jax.random.split(keys[4], owners))
        return (target * BR + offsets[target, order]).reshape(BRICKS)
    return jax.vmap(one_scene)(jax.random.split(key, SCENES)).astype(jnp.int32)


def steps_of(stream_key, dims, pieces, least, high):
    def one(dim, shards_of):
        heights = jax.random.uniform(jax.random.fold_in(jax.random.fold_in(stream_key, 6), dim), (shards_of,), jnp.float32, least / len(pieces), high / len(pieces))
        return jnp.repeat(jnp.exp(heights), dims[dim] // shards_of).reshape((-1,) + (1,) * (len(dims) - dim - 1))

    factor_of = one(*pieces[0])
    for cut in pieces[1:]:
        factor_of = factor_of * one(*cut)
    return factor_of


def centred(key, extent, scale, bound, cuts=(), kind=jnp.bfloat16):
    level = steps_of(key, extent, cuts, -0.22, 0.18) if cuts else 1.0
    values = jax.random.normal(key, extent, jnp.float32) * scale * level
    return jnp.minimum(jnp.maximum(values, -bound), bound).astype(kind)


def setup_inputs(seed: int = 0) -> dict:
    key_list = jax.random.split(jax.random.key(seed), 7)
    features = centred(key_list[0], (2, SCENES, BRICKS, 512, C), 1.0, 6.0, ((0, 2), (1, 4), (2, 4)))
    weights = centred(key_list[1], (2, 27, C, C), (27 * C) ** -0.5, 0.109375, ((0, 2),))
    projection = centred(key_list[2], (C, C), C ** -0.5, 0.5)
    cotangent = centred(key_list[3], (2, SCENES, BRICKS, 512, C), ((512 * SCENES * BRICKS) ** -0.5), 0.078125, ((0, 2), (1, 4), (2, 4)))
    neighbours = draw_neighbours(jax.random.fold_in(key_list[6], 71), 0)
    route = draw_route(jax.random.fold_in(key_list[6], 71), 0)
    return dict(features=features, weights=weights, projection=projection, cotangent=cotangent, neighbours=neighbours, route=route)


tap_moves = tuple((move_a, move_b, move_c) for move_a in (-1, 0, 1) for move_b in (-1, 0, 1) for move_c in (-1, 0, 1))
source_part = {-1: slice(7, 8), 0: slice(0, 8), 1: slice(0, 1)}
target_part = {-1: slice(0, 1), 0: slice(1, 9), 1: slice(9, 10)}


def silu_slope(values):
    sigmoid_part = jax.nn.sigmoid(values)
    return sigmoid_part * (1.0 + values * (1.0 - sigmoid_part))


def pad_bricks(bricks_grid, neighbour_rows):
    bricks_total = bricks_grid.shape[0]
    channels = bricks_grid.shape[-1]
    linkage = jnp.where(neighbour_rows >= 0, neighbour_rows, bricks_total).astype(jnp.int32)
    linkage = jnp.concatenate([linkage, jnp.full((1, 6), bricks_total, jnp.int32)], 0)
    padded = jnp.zeros((bricks_total, 10, 10, 10, channels), bricks_grid.dtype)
    padded = padded.at[:, 1:9, 1:9, 1:9].set(bricks_grid)
    for tap_move in tap_moves:
        step_a, step_b, step_c = tap_move
        if step_a == 0 and step_b == 0 and step_c == 0:
            continue
        chain_rows = jnp.arange(bricks_total, dtype=jnp.int32)
        if step_c != 0:
            chain_rows = linkage[chain_rows, 4 if step_c > 0 else 5]
        if step_b != 0:
            chain_rows = linkage[chain_rows, 2 if step_b > 0 else 3]
        if step_a != 0:
            chain_rows = linkage[chain_rows, 0 if step_a > 0 else 1]
        region = bricks_grid[:, source_part[step_a], source_part[step_b], source_part[step_c]]
        region = jnp.concatenate([region, jnp.zeros((1,) + region.shape[1:], bricks_grid.dtype)], 0)
        padded = padded.at[:, target_part[step_a], target_part[step_b], target_part[step_c]].set(region[chain_rows])
    return padded


def tap_block(padded, tap_move):
    start_a, start_b, start_c = tap_move[0] + 1, tap_move[1] + 1, tap_move[2] + 1
    block = padded[:, start_a:start_a + 8, start_b:start_b + 8, start_c:start_c + 8]
    return block.reshape(-1, padded.shape[-1])


def apply_taps(padded, section_weights):
    summed = jnp.zeros((padded.shape[0] * 512, section_weights.shape[-1]), jnp.float32)
    for tap_index, tap_move in enumerate(tap_moves):
        summed = summed + jnp.dot(tap_block(padded, tap_move), section_weights[tap_index], preferred_element_type=jnp.float32)
    return summed


def tap_gradients(padded, slope_rows):
    return jnp.stack([lax.dot_general(tap_block(padded, tap_move), slope_rows, (((0,), (0,)), ((), ())), preferred_element_type=jnp.float32) for tap_move in tap_moves])


def reference(features, weights, projection, cotangent, neighbours, route):
    channels = features.shape[-1]
    weight_grads = jnp.zeros((2, 27, channels, channels), jnp.float32)
    projection_grad = jnp.zeros((channels, channels), jnp.float32)
    encoder_list = []
    decoder_list = []
    for scene in range(SCENES):
        enc_padded = pad_bricks(features[0, scene].reshape(BRICKS, 8, 8, 8, channels), neighbours[0, scene])
        enc_taps = apply_taps(enc_padded, weights[0])
        skip_tiles = jax.nn.silu(enc_taps).astype(jnp.bfloat16).reshape(BRICKS, 512, channels)
        skip_decoder = jnp.zeros_like(skip_tiles).at[route[scene]].set(skip_tiles)
        skip_flat = skip_decoder.reshape(-1, channels)
        dec_padded = pad_bricks(features[1, scene].reshape(BRICKS, 8, 8, 8, channels), neighbours[1, scene])
        dec_input = apply_taps(dec_padded, weights[1]) + jnp.dot(skip_flat, projection, preferred_element_type=jnp.float32)
        dec_output = jax.nn.silu(dec_input).astype(jnp.bfloat16)
        dec_slope = (cotangent[1, scene].reshape(-1, channels).astype(jnp.float32) * silu_slope(dec_input)).astype(jnp.bfloat16)
        skip_back = jnp.dot(dec_slope, projection.T, preferred_element_type=jnp.float32).astype(jnp.bfloat16)
        enc_back = skip_back.reshape(BRICKS, 512, channels)[route[scene]].reshape(-1, channels)
        enc_slope = ((cotangent[0, scene].reshape(-1, channels).astype(jnp.float32) + enc_back.astype(jnp.float32)) * silu_slope(enc_taps)).astype(jnp.bfloat16)
        weight_grads = weight_grads + jnp.stack([tap_gradients(enc_padded, enc_slope), tap_gradients(dec_padded, dec_slope)])
        projection_grad = projection_grad + lax.dot_general(skip_flat, dec_slope, (((0,), (0,)), ((), ())), preferred_element_type=jnp.float32)
        encoder_list.append(skip_tiles)
        decoder_list.append(dec_output.reshape(BRICKS, 512, channels))
    activations = jnp.stack([jnp.stack(encoder_list), jnp.stack(decoder_list)])
    return activations, weight_grads, projection_grad
```

```python
import functools

import jax
import jax.numpy as jnp
from jax import lax
from jax.experimental import pallas as pl
from jax.experimental.pallas import tpu as pltpu
from jax.sharding import PartitionSpec as P

MESH = pl.DeviceIdType.MESH
f32, bf16 = jnp.float32, jnp.bfloat16
VM = pl.BlockSpec(memory_space=pltpu.VMEM)
SM = pl.BlockSpec(memory_space=pltpu.SMEM)
LIMIT = 56 * 1024 * 1024


def params(collective=None):
    if collective is None:
        return pltpu.CompilerParams(vmem_limit_bytes=LIMIT)
    return pltpu.CompilerParams(
        vmem_limit_bytes=LIMIT, collective_id=collective, has_side_effects=True
    )


def halo_kernel(owners, feats, route, before, after, routes, s_up, r_up, s_dn, r_dn, s_rt, r_rt):
    me = lax.axis_index("brick")
    barrier = pltpu.get_barrier_semaphore()
    for k in range(1, owners):
        pl.semaphore_signal(
            barrier, inc=1, device_id={"brick": lax.rem(me + k, owners)}, device_id_type=MESH
        )
    pl.semaphore_wait(barrier, owners - 1)
    up = pltpu.make_async_remote_copy(
        src_ref=feats.at[:, 7], dst_ref=before, send_sem=s_up, recv_sem=r_up,
        device_id={"brick": lax.rem(me + 1, owners)}, device_id_type=MESH,
    )
    down = pltpu.make_async_remote_copy(
        src_ref=feats.at[:, 0], dst_ref=after, send_sem=s_dn, recv_sem=r_dn,
        device_id={"brick": lax.rem(me + owners - 1, owners)}, device_id_type=MESH,
    )
    up.start()
    down.start()
    sends = []
    for k in range(1, owners):
        copy = pltpu.make_async_remote_copy(
            src_ref=route, dst_ref=routes.at[me], send_sem=s_rt.at[k], recv_sem=r_rt.at[k],
            device_id={"brick": lax.rem(me + k, owners)}, device_id_type=MESH,
        )
        copy.start()
        sends.append(copy)
    routes[me] = route[...]
    for copy in sends:
        copy.wait()
    up.wait()
    down.wait()


def conv_kernel(
    owners, cap, nb, routes, feats, before, after, weights,
    taps, slots, z, tables, full, plus, minus, ext, wide, links,
):
    me = lax.axis_index("brick")
    bricks = feats.shape[0]
    start = me * bricks
    for r in range(bricks):
        up = nb[r, 0]
        dn = nb[r, 1]
        links[r, 0] = jnp.where(up >= 0, up - start, 2 * bricks)
        links[r, 1] = jnp.where(
            dn >= 0, jnp.where(dn >= start, dn - start, dn - start + 2 * bricks), 2 * bricks
        )
        for e in range(2, 6):
            links[r, e] = jnp.where(nb[r, e] >= 0, nb[r, e] - start, bricks)
    for e in range(6):
        links[bricks, e] = jnp.int32(2 * bricks if e < 2 else bricks)
    for i in range(owners * cap):
        tables[2, i] = jnp.int32(0)

    def one_owner(s, carry):
        targets = [lax.div(routes[s, r], bricks) for r in range(bricks)]
        for r in range(bricks):
            count = jnp.int32(0)
            for e in range(r):
                count = count + jnp.where(targets[e] == targets[r], 1, 0)

            @pl.when(s == me)
            def _():
                tables[0, r] = targets[r] * cap + count

            @pl.when(targets[r] == me)
            def _():
                row = lax.rem(routes[s, r], bricks)
                tables[1, row] = s * cap + count
                tables[2, s * cap + count] = row

        return carry

    lax.fori_loop(0, owners, one_owner, 0)

    for p in range(3):
        wide[:, p * 128 : (p + 1) * 128] = weights[9 * p : 9 * p + 9].reshape(1152, 128)
    full[:bricks] = feats[...].astype(f32)
    full[bricks] = jnp.zeros(full.shape[1:], f32)
    plus[:bricks] = feats[:, 0].astype(f32)
    plus[bricks : 2 * bricks] = after[...].astype(f32)
    plus[2 * bricks] = jnp.zeros(plus.shape[1:], f32)
    minus[:bricks] = feats[:, 7].astype(f32)
    minus[bricks : 2 * bricks] = before[...].astype(f32)
    minus[2 * bricks] = jnp.zeros(minus.shape[1:], f32)

    def shifted(t, inside, side):
        if t == 0:
            return inside
        axis = inside.ndim - 2
        place = lax.broadcasted_iota(jnp.int32, inside.shape, axis)
        joined = jnp.where(place == (0 if t > 0 else 7), side, inside)
        return pltpu.roll(joined, 7 if t > 0 else 1, axis)

    def one_brick(r, carry):
        r1 = {0: r, 1: links[r, 4], -1: links[r, 5]}
        r2 = {}
        for t in (-1, 0, 1):
            r2[0, t] = r1[t]
            r2[1, t] = links[r1[t], 2]
            r2[-1, t] = links[r1[t], 3]
        r3 = {}
        for q, t in r2:
            r3[1, q, t] = links[r2[q, t], 0]
            r3[-1, q, t] = links[r2[q, t], 1]
        for t in (-1, 0, 1):
            ext[t + 1, 1:9, 1:9] = shifted(t, full[r], full[r1[t]])
            ext[t + 1, 1:9, 0] = shifted(t, full[r2[-1, 0], :, 7], full[r2[-1, t], :, 7])
            ext[t + 1, 1:9, 9] = shifted(t, full[r2[1, 0], :, 0], full[r2[1, t], :, 0])
            for p, table in ((-1, minus), (1, plus)):
                a = 0 if p < 0 else 9
                ext[t + 1, a, 1:9] = shifted(t, table[r3[p, 0, 0]], table[r3[p, 0, t]])
                ext[t + 1, a, 0] = shifted(t, table[r3[p, -1, 0], 7], table[r3[p, -1, t], 7])
                ext[t + 1, a, 9] = shifted(t, table[r3[p, 1, 0], 0], table[r3[p, 1, t], 0])
        for q in range(3):
            for t in range(3):
                lane = (3 * q + t) * 128
                z[r, :, lane : lane + 128] = (
                    ext[t, :, q : q + 8].reshape(640, 128).astype(bf16)
                )
        product = jnp.dot(z[r], wide[...], preferred_element_type=f32)
        total = product[0:512, 0:128] + product[64:576, 128:256] + product[128:640, 256:384]
        taps[r] = total
        slots[tables[0, r]] = (total / (1.0 + jnp.exp(-total))).astype(bf16)
        return carry

    lax.fori_loop(0, bricks, one_brick, 0)


def skip_kernel(
    owners, cap, tables, taps, slots, projection, cotangent,
    acts, slope, skip, arrived, back, s_sem, r_sem, s_bk, r_bk,
):
    me = lax.axis_index("brick")
    section = lax.axis_index("section")
    bricks = taps.shape[0]
    barrier = pltpu.get_barrier_semaphore()
    for d in range(owners):
        pl.semaphore_signal(
            barrier, inc=1, device_id={"brick": d, "section": 1 - section}, device_id_type=MESH
        )
    pl.semaphore_wait(barrier, owners)

    def move(k, source, sends, receives):
        peer = lax.rem(me + k, owners)
        return pltpu.make_async_remote_copy(
            src_ref=source.at[pl.ds(peer * cap, cap)],
            dst_ref=arrived.at[pl.ds(me * cap, cap)],
            send_sem=sends.at[k], recv_sem=receives.at[k],
            device_id={"brick": peer, "section": 1 - section}, device_id_type=MESH,
        )

    order = [k for k in range(1, owners)] + [0]

    @pl.when(section == 0)
    def _():
        for k in order:
            move(k, slots, s_sem, r_sem).start()
        skip[...] = jnp.zeros(skip.shape, skip.dtype)

        def gate(r, carry):
            v = taps[r]
            acts[r] = (v / (1.0 + jnp.exp(-v))).astype(bf16)
            return carry

        lax.fori_loop(0, bricks, gate, 0)
        for k in order:
            move(k, slots, s_sem, r_sem).wait_send()
        for k in order:
            move(k, back, s_bk, r_bk).wait_recv()

        def last(r, carry):
            v = taps[r]
            g = 1.0 / (1.0 + jnp.exp(-v))
            both = cotangent[r].astype(f32) + arrived[tables[0, r]].astype(f32)
            slope[r] = (both * (g * (1.0 + v * (1.0 - g)))).astype(bf16)
            return carry

        lax.fori_loop(0, bricks, last, 0)

    @pl.when(section == 1)
    def _():
        for k in order:
            move(k, slots, s_sem, r_sem).wait_recv()

        def step(r, carry):
            tile = arrived[tables[1, r]]
            skip[r] = tile
            v = taps[r] + jnp.dot(tile, projection[...], preferred_element_type=f32)
            g = 1.0 / (1.0 + jnp.exp(-v))
            acts[r] = (v * g).astype(bf16)
            slope[r] = (cotangent[r].astype(f32) * (g * (1.0 + v * (1.0 - g)))).astype(bf16)
            return carry

        lax.fori_loop(0, bricks, step, 0)

        def pack(i, carry):
            back[i] = lax.dot_general(
                slope[tables[2, i]], projection[...], (((1,), (1,)), ((), ())),
                preferred_element_type=f32,
            ).astype(bf16)
            return carry

        lax.fori_loop(0, owners * cap, pack, 0)
        for k in order:
            move(k, back, s_bk, r_bk).start()
        for k in order:
            move(k, back, s_bk, r_bk).wait_send()


def grad_kernel(z, slope, skip, out, spread, total):
    bricks = z.shape[0]
    spread[...] = jnp.zeros(spread.shape, bf16)
    total[...] = jnp.zeros(total.shape, f32)

    def one(r, acc):
        for p in range(3):
            spread[p * 64 : p * 64 + 512, p * 128 : (p + 1) * 128] = slope[r]
        total[...] += lax.dot_general(
            z[r], spread[...], (((0,), (0,)), ((), ())), preferred_element_type=f32
        )
        return acc + lax.dot_general(
            skip[r], slope[r], (((0,), (0,)), ((), ())), preferred_element_type=f32
        )

    projected = lax.fori_loop(0, bricks, one, jnp.zeros((128, 128), f32))
    for p in range(3):
        out[1152 * p : 1152 * (p + 1)] = total[:, p * 128 : (p + 1) * 128].astype(bf16)
    out[3456:3584] = projected.astype(bf16)
    if out.shape[0] > 3584:
        out[3584:] = jnp.zeros((out.shape[0] - 3584, 128), bf16)


def sum_kernel(
    owners, scenes, grads, out, proj, rx1, part, rx2, s1, r1, s2, r2, s3, r3, s4, r4, s5, r5
):
    b = lax.axis_index("brick")
    z = lax.axis_index("dp")
    section = lax.axis_index("section")
    rows = grads.shape[0] // (owners * scenes)
    wide = rows * scenes
    barrier = pltpu.get_barrier_semaphore()
    for k in range(1, owners):
        pl.semaphore_signal(
            barrier, inc=1, device_id={"brick": lax.rem(b + k, owners)}, device_id_type=MESH
        )
    for k in range(1, scenes):
        pl.semaphore_signal(
            barrier, inc=1, device_id={"dp": lax.rem(z + k, scenes)}, device_id_type=MESH
        )
    pl.semaphore_signal(barrier, inc=1, device_id={"section": 1 - section}, device_id_type=MESH)
    pl.semaphore_wait(barrier, owners + scenes - 1)

    def chunk(ref, owner, scene):
        return ref.at[pl.ds(pl.multiple_of(owner * wide + scene * rows, 16), rows)]

    started = []

    def send(source, target, s, r, where):
        copy = pltpu.make_async_remote_copy(
            src_ref=source, dst_ref=target, send_sem=s, recv_sem=r,
            device_id=where, device_id_type=MESH,
        )
        copy.start()
        started.append(copy)
        return copy

    along = list(range(1, scenes)) + [0]
    first, second, third, fourth = {}, {}, {}, {}
    for j in along:
        scene = lax.rem(z + j, scenes)
        for k in range(1, owners):
            peer = lax.rem(b + k, owners)
            first[j, k] = send(
                chunk(grads, peer, scene), rx1.at[j, k], s1.at[j, k], r1.at[j, k], {"brick": peer}
            )
    for j in along:
        scene = lax.rem(z + j, scenes)
        for k in range(1, owners):
            first[j, k].wait_recv()
        mine = pl.multiple_of(b * wide + scene * rows, 16)
        summed = grads[pl.ds(mine, rows), :].astype(f32)
        for k in range(1, owners):
            summed = summed + rx1[j, k].astype(f32)
        if j:
            part[j] = summed.astype(bf16)
            second[j] = send(part.at[j], rx2.at[j], s2.at[j], r2.at[j], {"dp": scene})
    for j in range(1, scenes):
        second[j].wait_recv()
        summed = summed + rx2[j].astype(f32)
    mine = pl.multiple_of(b * wide + z * rows, 16)
    out[pl.ds(mine, rows), :] = summed.astype(bf16)
    for j in range(1, scenes):
        third[j] = send(
            chunk(out, b, z), chunk(out, b, z), s3.at[j], r3.at[j],
            {"dp": lax.rem(z + j, scenes)},
        )
    for j in range(scenes):
        scene = lax.rem(z + scenes - j, scenes)
        if j:
            third[j].wait_recv()
        for k in range(1, owners):
            fourth[j, k] = send(
                chunk(out, b, scene), chunk(out, b, scene), s4.at[j, k], r4.at[j, k],
                {"brick": lax.rem(b + k, owners)},
            )
    for copy in fourth.values():
        copy.wait_recv()
    last = pltpu.make_async_remote_copy(
        src_ref=out.at[pl.ds(3456, 128)], dst_ref=proj, send_sem=s5, recv_sem=r5,
        device_id={"section": 1 - section}, device_id_type=MESH,
    )

    @pl.when(section == 1)
    def _():
        last.start()
        proj[...] = out[3456:3584, :]
        last.wait_send()

    @pl.when(section == 0)
    def _():
        last.wait_recv()

    for copy in started:
        copy.wait_send()


def body(features, weights, projection, cotangent, neighbours, route):
    bricks, channels = features.shape[2], features.shape[-1]
    owners, scenes = lax.axis_size("brick"), lax.axis_size("dp")
    cap = max(2, 3 * bricks // (2 * owners))
    feats = features[0, 0].reshape(bricks, 8, 8, 8, channels)
    dma, arr = pltpu.SemaphoreType.DMA, jax.ShapeDtypeStruct
    route_tile = jnp.pad(route, ((0, 7), (0, 128 - bricks)))
    plane = (bricks, 8, 8, channels)
    before, after, routes = pl.pallas_call(
        functools.partial(halo_kernel, owners),
        out_shape=[arr(plane, bf16), arr(plane, bf16), arr((owners, 8, 128), jnp.int32)],
        in_specs=[VM, VM],
        out_specs=[VM, VM, VM],
        scratch_shapes=[dma, dma, dma, dma, dma((owners,)), dma((owners,))],
        compiler_params=params(0),
    )(feats, route_tile)

    count = owners * cap
    taps, slots, z, tables = pl.pallas_call(
        functools.partial(conv_kernel, owners, cap),
        out_shape=[
            arr((bricks, 512, channels), f32),
            arr((count, 512, channels), bf16),
            arr((bricks, 640, 9 * channels), bf16),
            arr((3, max(count, bricks)), jnp.int32),
        ],
        in_specs=[SM, SM, VM, VM, VM, VM],
        out_specs=[VM, VM, VM, SM],
        scratch_shapes=[
            pltpu.VMEM((bricks + 1, 8, 8, 8, channels), f32),
            pltpu.VMEM((2 * bricks + 1, 8, 8, channels), f32),
            pltpu.VMEM((2 * bricks + 1, 8, 8, channels), f32),
            pltpu.VMEM((3, 10, 10, 8, channels), f32),
            pltpu.VMEM((9 * channels, 3 * channels), bf16),
            pltpu.SMEM((bricks + 1, 6), jnp.int32),
        ],
        compiler_params=params(),
    )(neighbours[0, 0], routes[:, 0, :bricks], feats, before, after, weights[0])

    tile = (bricks, 512, channels)
    acts, slope, skip = pl.pallas_call(
        functools.partial(skip_kernel, owners, cap),
        out_shape=[arr(tile, bf16)] * 3,
        in_specs=[SM, VM, VM, VM, VM],
        out_specs=[VM, VM, VM],
        scratch_shapes=[
            pltpu.VMEM((count, 512, channels), bf16),
            pltpu.VMEM((count, 512, channels), bf16),
            dma((owners,)), dma((owners,)), dma((owners,)), dma((owners,)),
        ],
        compiler_params=params(1),
    )(tables, taps, slots, projection, cotangent[0, 0])

    unit = 16 * owners * scenes
    total = -(-28 * channels // unit) * unit
    grads = pl.pallas_call(
        grad_kernel,
        out_shape=arr((total, channels), bf16),
        in_specs=[VM, VM, VM],
        out_specs=VM,
        scratch_shapes=[
            pltpu.VMEM((640, 3 * channels), bf16),
            pltpu.VMEM((9 * channels, 3 * channels), f32),
        ],
        compiler_params=params(),
    )(z, slope, skip)

    rows = total // (owners * scenes)
    summed, projected = pl.pallas_call(
        functools.partial(sum_kernel, owners, scenes),
        out_shape=[arr((total, channels), bf16), arr((channels, channels), bf16)],
        in_specs=[VM],
        out_specs=[VM, VM],
        scratch_shapes=[
            pltpu.VMEM((scenes, owners, rows, channels), bf16),
            pltpu.VMEM((scenes, rows, channels), bf16),
            pltpu.VMEM((scenes, rows, channels), bf16),
            dma((scenes, owners)), dma((scenes, owners)),
            dma((scenes,)), dma((scenes,)),
            dma((scenes,)), dma((scenes,)),
            dma((scenes, owners)), dma((scenes, owners)),
            dma, dma,
        ],
        compiler_params=params(2),
    )(grads)
    return (
        acts[None, None],
        summed[: 27 * channels].astype(f32).reshape(1, 27, channels, channels),
        projected.astype(f32),
    )


def solution(mesh):
    return jax.shard_map(
        body,
        mesh=mesh,
        in_specs=(
            P("section", "dp", "brick", None, None),
            P("section", None, None, None),
            P(),
            P("section", "dp", "brick", None, None),
            P("section", "dp", "brick", None),
            P("dp", "brick"),
        ),
        out_specs=(P("section", "dp", "brick", None, None), P("section", None, None, None), P()),
        check_vma=False,
    )
```

```python
import functools

import jax
import jax.numpy as jnp
from jax import lax
from jax.experimental import pallas as pl
from jax.experimental.pallas import tpu as pltpu
from jax.sharding import PartitionSpec as P

MESH = pl.DeviceIdType.MESH
f32, bf16 = jnp.float32, jnp.bfloat16
VM = pl.BlockSpec(memory_space=pltpu.VMEM)
SM = pl.BlockSpec(memory_space=pltpu.SMEM)
LIMIT = 56 * 1024 * 1024


def params(collective=None):
    if collective is None:
        return pltpu.CompilerParams(vmem_limit_bytes=LIMIT)
    return pltpu.CompilerParams(
        vmem_limit_bytes=LIMIT, collective_id=collective, has_side_effects=True
    )


def halo_kernel(owners, feats, route, before, after, routes, s_up, r_up, s_dn, r_dn, s_rt, r_rt):
    me = lax.axis_index("brick")
    barrier = pltpu.get_barrier_semaphore()
    for k in range(1, owners):
        pl.semaphore_signal(
            barrier, inc=1, device_id={"brick": lax.rem(me + k, owners)}, device_id_type=MESH
        )
    pl.semaphore_wait(barrier, owners - 1)
    up = pltpu.make_async_remote_copy(
        src_ref=feats.at[:, 7], dst_ref=before, send_sem=s_up, recv_sem=r_up,
        device_id={"brick": lax.rem(me + 1, owners)}, device_id_type=MESH,
    )
    down = pltpu.make_async_remote_copy(
        src_ref=feats.at[:, 0], dst_ref=after, send_sem=s_dn, recv_sem=r_dn,
        device_id={"brick": lax.rem(me + owners - 1, owners)}, device_id_type=MESH,
    )
    up.start()
    down.start()
    sends = []
    for k in range(1, owners):
        copy = pltpu.make_async_remote_copy(
            src_ref=route, dst_ref=routes.at[me], send_sem=s_rt.at[k], recv_sem=r_rt.at[k],
            device_id={"brick": lax.rem(me + k, owners)}, device_id_type=MESH,
        )
        copy.start()
        sends.append(copy)
    routes[me] = route[...]
    for copy in sends:
        copy.wait()
    up.wait()
    down.wait()


def conv_kernel(
    owners, cap, nb, routes, feats, before, after, weights,
    taps, slots, z, tables, full, plus, minus, ext, wide, links,
):
    me = lax.axis_index("brick")
    bricks = feats.shape[0]
    start = me * bricks
    for r in range(bricks):
        up = nb[r, 0]
        dn = nb[r, 1]
        links[r, 0] = jnp.where(up >= 0, up - start, 2 * bricks)
        links[r, 1] = jnp.where(
            dn >= 0, jnp.where(dn >= start, dn - start, dn - start + 2 * bricks), 2 * bricks
        )
        for e in range(2, 6):
            links[r, e] = jnp.where(nb[r, e] >= 0, nb[r, e] - start, bricks)
    for e in range(6):
        links[bricks, e] = jnp.int32(2 * bricks if e < 2 else bricks)
    for i in range(owners * cap):
        tables[2, i] = jnp.int32(0)

    def one_owner(s, carry):
        targets = [lax.div(routes[s, 0, r], bricks) for r in range(bricks)]
        for r in range(bricks):
            count = jnp.int32(0)
            for e in range(r):
                count = count + jnp.where(targets[e] == targets[r], 1, 0)

            @pl.when(s == me)
            def _():
                tables[0, r] = targets[r] * cap + count

            @pl.when(targets[r] == me)
            def _():
                row = lax.rem(routes[s, 0, r], bricks)
                tables[1, row] = s * cap + count
                tables[2, s * cap + count] = row

        return carry

    lax.fori_loop(0, owners, one_owner, 0)

    for p in range(3):
        wide[:, p * 128 : (p + 1) * 128] = weights[9 * p : 9 * p + 9].reshape(1152, 128)
    full[:bricks] = feats[...].astype(f32)
    full[bricks] = jnp.zeros(full.shape[1:], f32)
    plus[:bricks] = feats[:, 0].astype(f32)
    plus[bricks : 2 * bricks] = after[...].astype(f32)
    plus[2 * bricks] = jnp.zeros(plus.shape[1:], f32)
    minus[:bricks] = feats[:, 7].astype(f32)
    minus[bricks : 2 * bricks] = before[...].astype(f32)
    minus[2 * bricks] = jnp.zeros(minus.shape[1:], f32)

    def shifted(t, inside, side):
        if t == 0:
            return inside
        axis = inside.ndim - 2
        place = lax.broadcasted_iota(jnp.int32, inside.shape, axis)
        joined = jnp.where(place == (0 if t > 0 else 7), side, inside)
        return pltpu.roll(joined, 7 if t > 0 else 1, axis)

    def one_brick(r, carry):
        r1 = {0: r, 1: links[r, 4], -1: links[r, 5]}
        r2 = {}
        for t in (-1, 0, 1):
            r2[0, t] = r1[t]
            r2[1, t] = links[r1[t], 2]
            r2[-1, t] = links[r1[t], 3]
        r3 = {}
        for q, t in r2:
            r3[1, q, t] = links[r2[q, t], 0]
            r3[-1, q, t] = links[r2[q, t], 1]
        for t in (-1, 0, 1):
            ext[t + 1, 1:9, 1:9] = shifted(t, full[r], full[r1[t]])
            ext[t + 1, 1:9, 0] = shifted(t, full[r2[-1, 0], :, 7], full[r2[-1, t], :, 7])
            ext[t + 1, 1:9, 9] = shifted(t, full[r2[1, 0], :, 0], full[r2[1, t], :, 0])
            for p, table in ((-1, minus), (1, plus)):
                a = 0 if p < 0 else 9
                ext[t + 1, a, 1:9] = shifted(t, table[r3[p, 0, 0]], table[r3[p, 0, t]])
                ext[t + 1, a, 0] = shifted(t, table[r3[p, -1, 0], 7], table[r3[p, -1, t], 7])
                ext[t + 1, a, 9] = shifted(t, table[r3[p, 1, 0], 0], table[r3[p, 1, t], 0])
        for q in range(3):
            for t in range(3):
                lane = (3 * q + t) * 128
                z[r, :, lane : lane + 128] = (
                    ext[t, :, q : q + 8].reshape(640, 128).astype(bf16)
                )
        product = jnp.dot(z[r], wide[...], preferred_element_type=f32)
        total = product[0:512, 0:128] + product[64:576, 128:256] + product[128:640, 256:384]
        taps[r] = total
        slots[tables[0, r]] = (total / (1.0 + jnp.exp(-total))).astype(bf16)
        return carry

    lax.fori_loop(0, bricks, one_brick, 0)


def reduce_part(grads, out, base, outer, inner, rx1, part, rx2, sems, started):
    (outer_name, n1), (inner_name, n2) = outer, inner
    x, y = lax.axis_index(outer_name), lax.axis_index(inner_name)
    rows = rx2.shape[1]
    s1, r1, s2, r2, s3, r3, s4, r4 = sems

    def chunk(ref, i, j):
        return ref.at[pl.ds(pl.multiple_of(base + (i * n2 + j) * rows, 16), rows)]

    def load(ref, i, j):
        return ref[pl.ds(pl.multiple_of(base + (i * n2 + j) * rows, 16), rows), :]

    def send(source, target, s, r, where):
        copy = pltpu.make_async_remote_copy(
            src_ref=source, dst_ref=target, send_sem=s, recv_sem=r,
            device_id=where, device_id_type=MESH,
        )
        copy.start()
        started.append(copy)
        return copy

    def other(k):
        return lax.rem(x + k, n1)

    def along(j):
        return lax.rem(y + j, n2)

    order = list(range(1, n2)) + [0]
    first, second, third, fourth = {}, {}, {}, {}
    held = []

    def scatter():
        for j in order:
            for k in range(1, n1):
                first[j, k] = send(
                    chunk(grads, other(k), along(j)), rx1.at[j, k], s1.at[j, k], r1.at[j, k],
                    {outer_name: other(k)},
                )

    def forward(j):
        for k in range(1, n1):
            first[j, k].wait_recv()
        summed = load(grads, x, along(j)).astype(f32)
        for k in range(1, n1):
            summed = summed + rx1[j, k].astype(f32)
        part[j] = summed.astype(bf16) if j else jnp.zeros(part.shape[1:], bf16)
        if j:
            second[j] = send(
                part.at[j], rx2.at[j], s2.at[j], r2.at[j], {inner_name: along(j)}
            )
        else:
            held.append(summed)

    def spread_out(j, scene):
        for k in range(1, n1):
            fourth[j, k] = send(
                chunk(out, x, scene), chunk(out, x, scene), s4.at[j, k], r4.at[j, k],
                {outer_name: other(k)},
            )

    def finish():
        summed = held[0]
        for j in range(1, n2):
            second[j].wait_recv()
            summed = summed + rx2[j].astype(f32)
        out[pl.ds(pl.multiple_of(base + (x * n2 + y) * rows, 16), rows), :] = summed.astype(bf16)
        for j in range(1, n2):
            third[j] = send(
                chunk(out, x, y), chunk(out, x, y), s3.at[j], r3.at[j], {inner_name: along(j)}
            )
        spread_out(0, y)

    def gather(j):
        third[j].wait_recv()
        spread_out(j, lax.rem(y + n2 - j, n2))

    def end():
        for copy in fourth.values():
            copy.wait_recv()

    return scatter, forward, finish, gather, end, order


def back_kernel(
    owners, scenes, cap, split, tables, taps, slots, projection, cotangent, z_far,
    acts, out, proj,
    z, slope, skip, factor, lifted, arrived, back, spread, total, grads, rx, part,
    rx2a, rx2b, rx1b, partb, z_sem, s_sem, r_sem, s_bk, r_bk, *rest,
):
    me = lax.axis_index("brick")
    scene = lax.axis_index("dp")
    section = lax.axis_index("section")
    bricks = taps.shape[0]
    z_copy = pltpu.make_async_copy(z_far, z, z_sem)
    z_copy.start()
    barrier = pltpu.get_barrier_semaphore()
    for d in range(owners):
        pl.semaphore_signal(
            barrier, inc=1, device_id={"brick": d, "section": 1 - section}, device_id_type=MESH
        )
    for k in range(1, owners):
        pl.semaphore_signal(
            barrier, inc=1, device_id={"brick": lax.rem(me + k, owners)}, device_id_type=MESH
        )
    for k in range(1, scenes):
        pl.semaphore_signal(
            barrier, inc=1, device_id={"dp": lax.rem(scene + k, scenes)}, device_id_type=MESH
        )
    pl.semaphore_wait(barrier, 2 * owners - 1 + scenes - 1)

    pieces = s_sem.shape[0]
    height = 512 // pieces

    def move(c, k, source, sends, receives):
        peer = lax.rem(me + k, owners)
        return pltpu.make_async_remote_copy(
            src_ref=source.at[pl.ds(peer * cap, cap), pl.ds(c * height, height)],
            dst_ref=arrived[c].at[pl.ds(me * cap, cap)],
            send_sem=sends.at[c, k], recv_sem=receives.at[c, k],
            device_id={"brick": peer, "section": 1 - section}, device_id_type=MESH,
        )

    order = [k for k in range(1, owners)] + [0]

    @pl.when(section == 0)
    def _():
        for c in range(pieces):
            for k in order:
                move(c, k, slots, s_sem, r_sem).start()
        skip[...] = jnp.zeros(skip.shape, skip.dtype)

        def gate(r, carry):
            v = taps[r]
            g = 1.0 / (1.0 + jnp.exp(-v))
            acts[r] = (v * g).astype(bf16)
            factor[r] = g * (1.0 + v * (1.0 - g))
            return carry

        lax.fori_loop(0, bricks, gate, 0)
        for c in range(pieces):
            for k in order:
                move(c, k, back, s_bk, r_bk).wait_recv()
            span = slice(c * height, (c + 1) * height)

            def last(r, carry):
                both = cotangent[r, span].astype(f32) + arrived[c][tables[0, r]].astype(f32)
                slope[r, span] = (both * factor[r, span]).astype(bf16)
                return carry

            lax.fori_loop(0, bricks, last, 0)

    @pl.when(section == 1)
    def _():
        for c in range(pieces):
            for k in order:
                move(c, k, slots, s_sem, r_sem).wait_recv()
            span = slice(c * height, (c + 1) * height)

            def step(r, carry):
                tile = arrived[c][tables[1, r]]
                skip[r, span] = tile
                v = taps[r, span] + jnp.dot(tile, projection[...], preferred_element_type=f32)
                g = 1.0 / (1.0 + jnp.exp(-v))
                acts[r, span] = (v * g).astype(bf16)
                down = (cotangent[r, span].astype(f32) * (g * (1.0 + v * (1.0 - g)))).astype(bf16)
                slope[r, span] = down
                lifted[r, span] = lax.dot_general(
                    down, projection[...], (((1,), (1,)), ((), ())), preferred_element_type=f32
                ).astype(bf16)
                return carry

            lax.fori_loop(0, bricks, step, 0)

            def pack(i, carry):
                back[i, span] = lifted[tables[2, i], span]
                return carry

            lax.fori_loop(0, owners * cap, pack, 0)
            for k in order:
                move(c, k, back, s_bk, r_bk).start()

    z_copy.wait()
    spread[...] = jnp.zeros(spread.shape, bf16)
    total[...] = jnp.zeros(total.shape, f32)

    def one(r, acc):
        for p in range(3):
            spread[p * 64 : p * 64 + 512, p * 128 : (p + 1) * 128] = slope[r]
        total[...] += lax.dot_general(
            z[r], spread[...], (((0,), (0,)), ((), ())), preferred_element_type=f32
        )
        return acc + lax.dot_general(
            skip[r], slope[r], (((0,), (0,)), ((), ())), preferred_element_type=f32
        )

    projected = lax.fori_loop(0, bricks, one, jnp.zeros((128, 128), f32))
    for p in range(3):
        grads[1152 * p : 1152 * (p + 1)] = total[:, p * 128 : (p + 1) * 128].astype(bf16)
    grads[3456:3584] = projected.astype(bf16)
    if grads.shape[0] > 3584:
        grads[3584:] = jnp.zeros((grads.shape[0] - 3584, 128), bf16)

    started = []
    on_brick, on_dp = ("brick", owners), ("dp", scenes)
    one_part = reduce_part(grads, out, 0, on_brick, on_dp, rx, part, rx2a, rest[:8], started)
    two_part = reduce_part(
        grads, out, split, on_dp, on_brick, rx1b, partb, rx2b, rest[8:16], started
    )
    both = (one_part, two_part)
    for way in both:
        way[0]()
    for i in range(max(owners, scenes)):
        for way in both:
            if i < len(way[5]):
                way[1](way[5][i])
    for way in both:
        way[2]()
    for i in range(1, max(owners, scenes)):
        for way in both:
            if i < len(way[5]):
                way[3](i)
    for way in both:
        way[4]()
    s5, r5 = rest[16:18]
    last_copy = pltpu.make_async_remote_copy(
        src_ref=out.at[pl.ds(3456, 128)], dst_ref=proj, send_sem=s5, recv_sem=r5,
        device_id={"section": 1 - section}, device_id_type=MESH,
    )

    @pl.when(section == 1)
    def _():
        last_copy.start()
        proj[...] = out[3456:3584, :]
        last_copy.wait_send()
        for c in range(pieces):
            for k in order:
                move(c, k, back, s_bk, r_bk).wait_send()

    @pl.when(section == 0)
    def _():
        last_copy.wait_recv()
        for c in range(pieces):
            for k in order:
                move(c, k, slots, s_sem, r_sem).wait_send()

    for copy in started:
        copy.wait_send()


def tail_kernel(summed, projected, acts, weight_out, proj_out, acts_out):
    weight_out[...] = summed[...].astype(f32)
    proj_out[...] = projected[...].astype(f32)
    acts_out[...] = acts[...]


def body(features, weights, projection, cotangent, neighbours, route):
    bricks, channels = features.shape[2], features.shape[-1]
    owners, scenes = lax.axis_size("brick"), lax.axis_size("dp")
    cap = max(2, 3 * bricks // (2 * owners))
    feats = features[0, 0].reshape(bricks, 8, 8, 8, channels)
    dma, arr = pltpu.SemaphoreType.DMA, jax.ShapeDtypeStruct
    plane = (bricks, 8, 8, channels)
    before, after, routes = pl.pallas_call(
        functools.partial(halo_kernel, owners),
        out_shape=[arr(plane, bf16), arr(plane, bf16), arr((owners, 1, bricks), jnp.int32)],
        in_specs=[VM, VM],
        out_specs=[VM, VM, VM],
        scratch_shapes=[dma, dma, dma, dma, dma((owners,)), dma((owners,))],
        compiler_params=params(0),
    )(feats, route)

    count = owners * cap
    taps, slots, z, tables = pl.pallas_call(
        functools.partial(conv_kernel, owners, cap),
        out_shape=[
            arr((bricks, 512, channels), f32),
            arr((count, 512, channels), bf16),
            arr((bricks, 640, 9 * channels), bf16),
            arr((3, max(count, bricks)), jnp.int32),
        ],
        in_specs=[SM, SM, VM, VM, VM, VM],
        out_specs=[VM, VM, VM, SM],
        scratch_shapes=[
            pltpu.VMEM((bricks + 1, 8, 8, 8, channels), f32),
            pltpu.VMEM((2 * bricks + 1, 8, 8, channels), f32),
            pltpu.VMEM((2 * bricks + 1, 8, 8, channels), f32),
            pltpu.VMEM((3, 10, 10, 8, channels), f32),
            pltpu.VMEM((9 * channels, 3 * channels), bf16),
            pltpu.SMEM((bricks + 1, 6), jnp.int32),
        ],
        compiler_params=params(),
    )(neighbours[0, 0], routes, feats, before, after, weights[0])

    tile = (bricks, 512, channels)
    unit = 16 * owners * scenes
    units = -(-28 * channels // unit)
    total = units * unit
    split = (2 * units + 2) // 3 * unit
    height_a, height_b = split // (owners * scenes), (total - split) // (owners * scenes)
    pieces = 4
    vm = pltpu.VMEM
    acts, summed, projected = pl.pallas_call(
        functools.partial(back_kernel, owners, scenes, cap, split),
        out_shape=[
            arr(tile, bf16), arr((total, channels), bf16), arr((channels, channels), bf16)
        ],
        in_specs=[SM, VM, VM, VM, VM, pl.BlockSpec(memory_space=pl.ANY)],
        out_specs=[VM, VM, VM],
        scratch_shapes=[
            vm(z.shape, bf16), vm(tile, bf16), vm(tile, bf16), vm(tile, f32), vm(tile, bf16),
            [vm((count, 512 // pieces, channels), bf16) for _ in range(pieces)],
            vm((count, 512, channels), bf16),
            vm((640, 3 * channels), bf16), vm((9 * channels, 3 * channels), f32),
            vm((total, channels), bf16),
            vm((scenes, owners, height_a, channels), bf16),
            vm((scenes, height_a, channels), bf16),
            vm((scenes, height_a, channels), bf16),
            vm((owners, height_b, channels), bf16),
            vm((owners, scenes, height_b, channels), bf16),
            vm((owners, height_b, channels), bf16),
            dma,
            *[dma((pieces, owners)) for _ in range(4)],
            dma((scenes, owners)), dma((scenes, owners)),
            *[dma((scenes,)) for _ in range(4)],
            dma((scenes, owners)), dma((scenes, owners)),
            dma((owners, scenes)), dma((owners, scenes)),
            *[dma((owners,)) for _ in range(4)],
            dma((owners, scenes)), dma((owners, scenes)),
            dma, dma,
        ],
        compiler_params=params(1),
    )(tables, taps, slots, projection, cotangent[0, 0], z)

    piece = 27 * channels // bricks
    weight_sum, projection_sum, acts = pl.pallas_call(
        tail_kernel,
        grid=(bricks,),
        out_shape=[
            arr((27 * channels, channels), f32), arr((channels, channels), f32), arr(tile, bf16)
        ],
        in_specs=[
            pl.BlockSpec((piece, channels), lambda i: (i, 0)),
            pl.BlockSpec((channels, channels), lambda i: (0, 0)),
            pl.BlockSpec((1, 512, channels), lambda i: (i, 0, 0)),
        ],
        out_specs=[
            pl.BlockSpec((piece, channels), lambda i: (i, 0)),
            pl.BlockSpec((channels, channels), lambda i: (0, 0)),
            pl.BlockSpec((1, 512, channels), lambda i: (i, 0, 0)),
        ],
        compiler_params=params(),
    )(summed, projected, acts)
    return (
        acts[None, None],
        weight_sum.reshape(1, 27, channels, channels),
        projection_sum,
    )


def solution(mesh):
    return jax.shard_map(
        body,
        mesh=mesh,
        in_specs=(
            P("section", "dp", "brick", None, None),
            P("section", None, None, None),
            P(),
            P("section", "dp", "brick", None, None),
            P("section", "dp", "brick", None),
            P("dp", "brick"),
        ),
        out_specs=(P("section", "dp", "brick", None, None), P("section", None, None, None), P()),
        check_vma=False,
    )
```

```python
import functools

import jax
import jax.numpy as jnp
from jax import lax
from jax.experimental import pallas as pl
from jax.experimental.pallas import tpu as pltpu
from jax.sharding import PartitionSpec as P

MESH = pl.DeviceIdType.MESH
f32, bf16 = jnp.float32, jnp.bfloat16
VM = pl.BlockSpec(memory_space=pltpu.VMEM)
SM = pl.BlockSpec(memory_space=pltpu.SMEM)
LIMIT = 56 * 1024 * 1024


def params(collective=None):
    if collective is None:
        return pltpu.CompilerParams(vmem_limit_bytes=LIMIT)
    return pltpu.CompilerParams(
        vmem_limit_bytes=LIMIT, collective_id=collective, has_side_effects=True
    )


def reduce_part(grads, out, base, outer, inner, rx1, part, rx2, sems, started):
    (outer_name, n1), (inner_name, n2) = outer, inner
    x, y = lax.axis_index(outer_name), lax.axis_index(inner_name)
    rows = rx2.shape[1]
    s1, r1, s2, r2, s3, r3, s4, r4 = sems

    def chunk(ref, i, j):
        return ref.at[pl.ds(pl.multiple_of(base + (i * n2 + j) * rows, 16), rows)]

    def load(ref, i, j):
        return ref[pl.ds(pl.multiple_of(base + (i * n2 + j) * rows, 16), rows), :]

    def send(source, target, s, r, where):
        copy = pltpu.make_async_remote_copy(
            src_ref=source, dst_ref=target, send_sem=s, recv_sem=r,
            device_id=where, device_id_type=MESH,
        )
        copy.start()
        started.append(copy)
        return copy

    def other(k):
        return lax.rem(x + k, n1)

    def along(j):
        return lax.rem(y + j, n2)

    order = list(range(1, n2)) + [0]
    first, second, third, fourth = {}, {}, {}, {}
    held = []

    def scatter():
        for j in order:
            for k in range(1, n1):
                first[j, k] = send(
                    chunk(grads, other(k), along(j)), rx1.at[j, k], s1.at[j, k], r1.at[j, k],
                    {outer_name: other(k)},
                )

    def forward(j):
        for k in range(1, n1):
            first[j, k].wait_recv()
        summed = load(grads, x, along(j)).astype(f32)
        for k in range(1, n1):
            summed = summed + rx1[j, k].astype(f32)
        part[j] = summed.astype(bf16) if j else jnp.zeros(part.shape[1:], bf16)
        if j:
            second[j] = send(
                part.at[j], rx2.at[j], s2.at[j], r2.at[j], {inner_name: along(j)}
            )
        else:
            held.append(summed)

    def spread_out(j, scene):
        for k in range(1, n1):
            fourth[j, k] = send(
                chunk(out, x, scene), chunk(out, x, scene), s4.at[j, k], r4.at[j, k],
                {outer_name: other(k)},
            )

    def finish():
        summed = held[0]
        for j in range(1, n2):
            second[j].wait_recv()
            summed = summed + rx2[j].astype(f32)
        out[pl.ds(pl.multiple_of(base + (x * n2 + y) * rows, 16), rows), :] = summed.astype(bf16)
        for j in range(1, n2):
            third[j] = send(
                chunk(out, x, y), chunk(out, x, y), s3.at[j], r3.at[j], {inner_name: along(j)}
            )
        spread_out(0, y)

    def gather(j):
        third[j].wait_recv()
        spread_out(j, lax.rem(y + n2 - j, n2))

    def end():
        for copy in fourth.values():
            copy.wait_recv()

    return scatter, forward, finish, gather, end, order


def shifted(t, inside, side):
    if t == 0:
        return inside
    axis = inside.ndim - 2
    place = lax.broadcasted_iota(jnp.int32, inside.shape, axis)
    joined = jnp.where(place == (0 if t > 0 else 7), side, inside)
    return pltpu.roll(joined, 7 if t > 0 else 1, axis)


def whole_kernel(
    owners, scenes, cap, split, nb, route, feats, weights, projection, cotangent,
    acts, out, proj,
    before, after, routes, routes_s, links, tables, full, plus, minus, ext, wide, taps, tiles, slots,
    z, slope, skip, factor, lifted, arrived, back, spread, total, grads, rx, part,
    rx2a, rx2b, rx1b, partb, s_up, r_up, s_dn, r_dn, s_rt, r_rt, rs_sem,
    s_sem, r_sem, s_bk, r_bk, *rest,
):
    me = lax.axis_index("brick")
    scene = lax.axis_index("dp")
    section = lax.axis_index("section")
    bricks = feats.shape[0]
    barrier = pltpu.get_barrier_semaphore()
    for d in range(owners):
        pl.semaphore_signal(
            barrier, inc=1, device_id={"brick": d, "section": 1 - section}, device_id_type=MESH
        )
    for k in range(1, owners):
        pl.semaphore_signal(
            barrier, inc=1, device_id={"brick": lax.rem(me + k, owners)}, device_id_type=MESH
        )
    for k in range(1, scenes):
        pl.semaphore_signal(
            barrier, inc=1, device_id={"dp": lax.rem(scene + k, scenes)}, device_id_type=MESH
        )
    routes[me] = route[...]
    start = me * bricks

    def inside(index, last):
        return jnp.minimum(jnp.maximum(index, 0), last)

    for r in range(bricks):
        up = nb[r, 0]
        dn = nb[r, 1]
        links[r, 0] = inside(jnp.where(up >= 0, up - start, 2 * bricks), 2 * bricks)
        back_row = jnp.where(dn >= start, dn - start, dn - start + 2 * bricks)
        links[r, 1] = inside(jnp.where(dn >= 0, back_row, 2 * bricks), 2 * bricks)
        for e in range(2, 6):
            links[r, e] = inside(jnp.where(nb[r, e] >= 0, nb[r, e] - start, bricks), bricks)
    for e in range(6):
        links[bricks, e] = jnp.int32(2 * bricks if e < 2 else bricks)
    full[:bricks] = feats[...].astype(f32)
    full[bricks] = jnp.zeros(full.shape[1:], f32)
    for p in range(3):
        wide[:, p * 128 : (p + 1) * 128] = weights[9 * p : 9 * p + 9].reshape(1152, 128)
    pl.semaphore_wait(barrier, 2 * owners - 1 + scenes - 1)

    halo = [
        pltpu.make_async_remote_copy(
            src_ref=feats.at[:, 7], dst_ref=before, send_sem=s_up, recv_sem=r_up,
            device_id={"brick": lax.rem(me + 1, owners)}, device_id_type=MESH,
        ),
        pltpu.make_async_remote_copy(
            src_ref=feats.at[:, 0], dst_ref=after, send_sem=s_dn, recv_sem=r_dn,
            device_id={"brick": lax.rem(me + owners - 1, owners)}, device_id_type=MESH,
        ),
    ]
    for k in range(1, owners):
        halo.append(
            pltpu.make_async_remote_copy(
                src_ref=route, dst_ref=routes.at[me], send_sem=s_rt.at[k], recv_sem=r_rt.at[k],
                device_id={"brick": lax.rem(me + k, owners)}, device_id_type=MESH,
            )
        )
    for copy in halo:
        copy.start()

    def chains(r):
        r1 = {0: r, 1: links[r, 4], -1: links[r, 5]}
        r2 = {}
        for t in (-1, 0, 1):
            r2[0, t] = r1[t]
            r2[1, t] = links[r1[t], 2]
            r2[-1, t] = links[r1[t], 3]
        return r1, r2

    def inner_planes(r, carry):
        r1, r2 = chains(r)
        for t in (-1, 0, 1):
            ext[t + 1, 1:9, 1:9] = shifted(t, full[r], full[r1[t]])
            ext[t + 1, 1:9, 0] = shifted(t, full[r2[-1, 0], :, 7], full[r2[-1, t], :, 7])
            ext[t + 1, 1:9, 9] = shifted(t, full[r2[1, 0], :, 0], full[r2[1, t], :, 0])
        for q in range(3):
            for t in range(3):
                lane = (3 * q + t) * 128
                z[r, 64:576, lane : lane + 128] = (
                    ext[t, 1:9, q : q + 8].reshape(512, 128).astype(bf16)
                )
        return carry

    lax.fori_loop(0, bricks, inner_planes, 0)
    plus[:bricks] = feats[:, 0].astype(f32)
    plus[2 * bricks] = jnp.zeros(plus.shape[1:], f32)
    minus[:bricks] = feats[:, 7].astype(f32)
    minus[2 * bricks] = jnp.zeros(minus.shape[1:], f32)
    for copy in halo:
        copy.wait_recv()
    route_copy = pltpu.make_async_copy(routes, routes_s, rs_sem)
    route_copy.start()
    plus[bricks : 2 * bricks] = after[...].astype(f32)
    minus[bricks : 2 * bricks] = before[...].astype(f32)

    def outer_planes(r, carry):
        r1, r2 = chains(r)
        for p, table in ((-1, minus), (1, plus)):
            a = 0 if p < 0 else 9
            r3 = {place: links[r2[place], 0 if p > 0 else 1] for place in r2}
            for t in (-1, 0, 1):
                ext[t + 1, a, 1:9] = shifted(t, table[r3[0, 0]], table[r3[0, t]])
                ext[t + 1, a, 0] = shifted(t, table[r3[-1, 0], 7], table[r3[-1, t], 7])
                ext[t + 1, a, 9] = shifted(t, table[r3[1, 0], 0], table[r3[1, t], 0])
            for q in range(3):
                for t in range(3):
                    lane = (3 * q + t) * 128
                    z[r, 64 * a : 64 * a + 64, lane : lane + 128] = (
                        ext[t, a, q : q + 8].reshape(64, 128).astype(bf16)
                    )
        product = jnp.dot(z[r], wide[...], preferred_element_type=f32)
        total_taps = product[0:512, 0:128] + product[64:576, 128:256] + product[128:640, 256:384]
        taps[r] = total_taps
        tiles[r] = (total_taps / (1.0 + jnp.exp(-total_taps))).astype(bf16)
        return carry

    lax.fori_loop(0, bricks, outer_planes, 0)
    route_copy.wait()

    def places(s):
        targets = [inside(lax.div(routes_s[s, 0, r], bricks), owners - 1) for r in range(bricks)]
        counts = []
        for r in range(bricks):
            count = jnp.int32(0)
            for e in range(r):
                count = count + jnp.where(targets[e] == targets[r], 1, 0)
            counts.append(jnp.minimum(count, cap - 1))
        return targets, counts

    targets, counts = places(me)
    mine = [targets[r] * cap + counts[r] for r in range(bricks)]
    for r in range(bricks):
        tables[0, r] = mine[r]
    for i in range(owners * cap):
        which = jnp.int32(0)
        for r in range(1, bricks):
            which = jnp.where(mine[r] == i, r, which)
        tables[3, i] = which

    def one_owner(s, found):
        targets, counts = places(s)
        found = list(found)
        rows = [inside(lax.rem(routes_s[s, 0, r], bricks), bricks - 1) for r in range(bricks)]
        for r in range(bricks):
            for row in range(bricks):
                hit = jnp.logical_and(targets[r] == me, rows[r] == row)
                found[row] = jnp.where(hit, s * cap + counts[r], found[row])
        for j in range(cap):
            tag = jnp.int32(0)
            for r in range(bricks):
                hit = jnp.logical_and(targets[r] == me, counts[r] == j)
                tag = jnp.where(hit, rows[r], tag)
            tables[2, s * cap + j] = tag
        return tuple(found)

    found = lax.fori_loop(0, owners, one_owner, (jnp.int32(0),) * bricks)
    for row in range(bricks):
        tables[1, row] = found[row]

    pieces = s_sem.shape[0]
    height = 512 // pieces

    def move(c, k, source, sends, receives):
        peer = lax.rem(me + k, owners)
        return pltpu.make_async_remote_copy(
            src_ref=source.at[pl.ds(peer * cap, cap), pl.ds(c * height, height)],
            dst_ref=arrived[c].at[pl.ds(me * cap, cap)],
            send_sem=sends.at[c, k], recv_sem=receives.at[c, k],
            device_id={"brick": peer, "section": 1 - section}, device_id_type=MESH,
        )

    order = [k for k in range(1, owners)] + [0]

    @pl.when(section == 0)
    def _():
        for c in range(pieces):
            span = slice(c * height, (c + 1) * height)

            def fill(i, carry):
                slots[i, span] = tiles[tables[3, i], span]
                return carry

            lax.fori_loop(0, owners * cap, fill, 0)
            for k in order:
                move(c, k, slots, s_sem, r_sem).start()
        skip[...] = jnp.zeros(skip.shape, skip.dtype)

        def gate(r, carry):
            v = taps[r]
            g = 1.0 / (1.0 + jnp.exp(-v))
            acts[r] = (v * g).astype(bf16)
            factor[r] = g * (1.0 + v * (1.0 - g))
            return carry

        lax.fori_loop(0, bricks, gate, 0)
        for c in range(pieces):
            for k in order:
                move(c, k, back, s_bk, r_bk).wait_recv()
            span = slice(c * height, (c + 1) * height)

            def last(r, carry):
                both = cotangent[r, span].astype(f32) + arrived[c][tables[0, r]].astype(f32)
                slope[r, span] = (both * factor[r, span]).astype(bf16)
                return carry

            lax.fori_loop(0, bricks, last, 0)

    @pl.when(section == 1)
    def _():
        for c in range(pieces):
            for k in order:
                move(c, k, slots, s_sem, r_sem).wait_recv()
            span = slice(c * height, (c + 1) * height)

            def step(r, carry):
                tile = arrived[c][tables[1, r]]
                skip[r, span] = tile
                v = taps[r, span] + jnp.dot(tile, projection[...], preferred_element_type=f32)
                g = 1.0 / (1.0 + jnp.exp(-v))
                acts[r, span] = (v * g).astype(bf16)
                down = (cotangent[r, span].astype(f32) * (g * (1.0 + v * (1.0 - g)))).astype(bf16)
                slope[r, span] = down
                lifted[r, span] = lax.dot_general(
                    down, projection[...], (((1,), (1,)), ((), ())), preferred_element_type=f32
                ).astype(bf16)
                return carry

            lax.fori_loop(0, bricks, step, 0)

            def pack(i, carry):
                back[i, span] = lifted[tables[2, i], span]
                return carry

            lax.fori_loop(0, owners * cap, pack, 0)
            for k in order:
                move(c, k, back, s_bk, r_bk).start()

    spread[...] = jnp.zeros(spread.shape, bf16)
    total[...] = jnp.zeros(total.shape, f32)

    def one(r, acc):
        for p in range(3):
            spread[p * 64 : p * 64 + 512, p * 128 : (p + 1) * 128] = slope[r]
        total[...] += lax.dot_general(
            z[r], spread[...], (((0,), (0,)), ((), ())), preferred_element_type=f32
        )
        return acc + lax.dot_general(
            skip[r], slope[r], (((0,), (0,)), ((), ())), preferred_element_type=f32
        )

    projected = lax.fori_loop(0, bricks, one, jnp.zeros((128, 128), f32))
    for p in range(3):
        grads[1152 * p : 1152 * (p + 1)] = total[:, p * 128 : (p + 1) * 128].astype(bf16)
    grads[3456:3584] = projected.astype(bf16)
    if grads.shape[0] > 3584:
        grads[3584:] = jnp.zeros((grads.shape[0] - 3584, 128), bf16)

    started = []
    on_brick, on_dp = ("brick", owners), ("dp", scenes)
    one_part = reduce_part(grads, out, 0, on_brick, on_dp, rx, part, rx2a, rest[:8], started)
    two_part = reduce_part(
        grads, out, split, on_dp, on_brick, rx1b, partb, rx2b, rest[8:16], started
    )
    both = (one_part, two_part)
    for way in both:
        way[0]()
    for i in range(max(owners, scenes)):
        for way in both:
            if i < len(way[5]):
                way[1](way[5][i])
    for way in both:
        way[2]()
    for i in range(1, max(owners, scenes)):
        for way in both:
            if i < len(way[5]):
                way[3](i)
    for way in both:
        way[4]()
    s5, r5 = rest[16:18]
    last_copy = pltpu.make_async_remote_copy(
        src_ref=out.at[pl.ds(3456, 128)], dst_ref=proj, send_sem=s5, recv_sem=r5,
        device_id={"section": 1 - section}, device_id_type=MESH,
    )

    @pl.when(section == 1)
    def _():
        last_copy.start()
        proj[...] = out[3456:3584, :]
        last_copy.wait_send()
        for c in range(pieces):
            for k in order:
                move(c, k, back, s_bk, r_bk).wait_send()

    @pl.when(section == 0)
    def _():
        last_copy.wait_recv()
        for c in range(pieces):
            for k in order:
                move(c, k, slots, s_sem, r_sem).wait_send()

    for copy in started:
        copy.wait_send()
    for copy in halo:
        copy.wait_send()


def tail_kernel(
    summed, projected, acts, weight_out, proj_out, acts_out,
    narrow, wider, proj_in, proj_wide, in_sem, out_sem, p_in, p_out, a_sem,
):
    pieces, rows = narrow.shape[:2]
    acts_copy = pltpu.make_async_copy(acts, acts_out, a_sem)
    fetch, store = [], []
    for c in range(pieces):
        span = pl.ds(c * rows, rows)
        fetch.append(pltpu.make_async_copy(summed.at[span], narrow.at[c], in_sem.at[c]))
        store.append(pltpu.make_async_copy(wider.at[c], weight_out.at[span], out_sem.at[c]))
        fetch[c].start()
    proj_fetch = pltpu.make_async_copy(projected, proj_in, p_in)
    proj_fetch.start()
    acts_copy.start()
    for c in range(pieces):
        fetch[c].wait()
        wider[c] = narrow[c].astype(f32)
        store[c].start()
    proj_fetch.wait()
    proj_wide[...] = proj_in[...].astype(f32)
    proj_store = pltpu.make_async_copy(proj_wide, proj_out, p_out)
    proj_store.start()
    for copy in store:
        copy.wait()
    proj_store.wait()
    acts_copy.wait()


def body(features, weights, projection, cotangent, neighbours, route):
    bricks, channels = features.shape[2], features.shape[-1]
    owners, scenes = lax.axis_size("brick"), lax.axis_size("dp")
    cap = max(2, 3 * bricks // (2 * owners))
    count = owners * cap
    feats = features[0, 0].reshape(bricks, 8, 8, 8, channels)
    dma, arr, vm = pltpu.SemaphoreType.DMA, jax.ShapeDtypeStruct, pltpu.VMEM
    plane = (bricks, 8, 8, channels)
    tile = (bricks, 512, channels)
    unit = 16 * owners * scenes
    units = -(-28 * channels // unit)
    total = units * unit
    split = (2 * units + 2) // 3 * unit
    height_a, height_b = split // (owners * scenes), (total - split) // (owners * scenes)
    pieces = 4
    anywhere = pl.BlockSpec(memory_space=pl.ANY)
    acts, summed, projected = pl.pallas_call(
        functools.partial(whole_kernel, owners, scenes, cap, split),
        out_shape=[
            arr(tile, bf16), arr((total, channels), bf16), arr((channels, channels), bf16)
        ],
        in_specs=[SM, VM, VM, VM, VM, VM],
        out_specs=[VM, VM, VM],
        scratch_shapes=[
            vm(plane, bf16), vm(plane, bf16), vm((owners, 1, bricks), jnp.int32),
            pltpu.SMEM((owners, 1, bricks), jnp.int32), pltpu.SMEM((bricks + 1, 6), jnp.int32),
            pltpu.SMEM((4, max(count, bricks)), jnp.int32),
            vm((bricks + 1, 8, 8, 8, channels), f32),
            vm((2 * bricks + 1, 8, 8, channels), f32),
            vm((2 * bricks + 1, 8, 8, channels), f32),
            vm((3, 10, 10, 8, channels), f32),
            vm((9 * channels, 3 * channels), bf16),
            vm(tile, f32), vm(tile, bf16), vm((count, 512, channels), bf16),
            vm((bricks, 640, 9 * channels), bf16),
            vm(tile, bf16), vm(tile, bf16), vm(tile, f32), vm(tile, bf16),
            [vm((count, 512 // pieces, channels), bf16) for _ in range(pieces)],
            vm((count, 512, channels), bf16),
            vm((640, 3 * channels), bf16), vm((9 * channels, 3 * channels), f32),
            vm((total, channels), bf16),
            vm((scenes, owners, height_a, channels), bf16),
            vm((scenes, height_a, channels), bf16),
            vm((scenes, height_a, channels), bf16),
            vm((owners, height_b, channels), bf16),
            vm((owners, scenes, height_b, channels), bf16),
            vm((owners, height_b, channels), bf16),
            dma, dma, dma, dma, dma((owners,)), dma((owners,)), dma,
            *[dma((pieces, owners)) for _ in range(4)],
            dma((scenes, owners)), dma((scenes, owners)),
            *[dma((scenes,)) for _ in range(4)],
            dma((scenes, owners)), dma((scenes, owners)),
            dma((owners, scenes)), dma((owners, scenes)),
            *[dma((owners,)) for _ in range(4)],
            dma((owners, scenes)), dma((owners, scenes)),
            dma, dma,
        ],
        compiler_params=params(0),
    )(neighbours[0, 0], route, feats, weights[0], projection, cotangent[0, 0])

    weight_sum, projection_sum, acts = pl.pallas_call(
        tail_kernel,
        out_shape=[
            arr((27 * channels, channels), f32), arr((channels, channels), f32), arr(tile, bf16)
        ],
        in_specs=[anywhere] * 3,
        out_specs=[anywhere] * 3,
        scratch_shapes=[
            vm((3, 9 * channels, channels), bf16), vm((3, 9 * channels, channels), f32),
            vm((channels, channels), bf16), vm((channels, channels), f32),
            dma((3,)), dma((3,)), dma, dma, dma,
        ],
        compiler_params=params(),
    )(summed, projected, acts)
    return (
        acts[None, None],
        weight_sum.reshape(1, 27, channels, channels),
        projection_sum,
    )


def solution(mesh):
    return jax.shard_map(
        body,
        mesh=mesh,
        in_specs=(
            P("section", "dp", "brick", None, None),
            P("section", None, None, None),
            P(),
            P("section", "dp", "brick", None, None),
            P("section", "dp", "brick", None),
            P("dp", "brick"),
        ),
        out_specs=(P("section", "dp", "brick", None, None), P("section", None, None, None), P()),
        check_vma=False,
    )
```

```python
import functools

import jax
import jax.numpy as jnp
from jax import lax
from jax.experimental import pallas as pl
from jax.experimental.pallas import tpu as pltpu
from jax.sharding import PartitionSpec as P

MESH = pl.DeviceIdType.MESH
f32, bf16 = jnp.float32, jnp.bfloat16
VM = pl.BlockSpec(memory_space=pltpu.VMEM)
SM = pl.BlockSpec(memory_space=pltpu.SMEM)
LIMIT = 56 * 1024 * 1024


def params(collective=None):
    if collective is None:
        return pltpu.CompilerParams(vmem_limit_bytes=LIMIT)
    return pltpu.CompilerParams(
        vmem_limit_bytes=LIMIT, collective_id=collective, has_side_effects=True
    )


def reduce_part(grads, out, base, outer, inner, rx1, part, rx2, sems, started):
    (outer_name, n1), (inner_name, n2) = outer, inner
    x, y = lax.axis_index(outer_name), lax.axis_index(inner_name)
    rows = rx2.shape[1]
    s1, r1, s2, r2, s3, r3, s4, r4 = sems

    def chunk(ref, i, j):
        return ref.at[pl.ds(pl.multiple_of(base + (i * n2 + j) * rows, 16), rows)]

    def load(ref, i, j):
        return ref[pl.ds(pl.multiple_of(base + (i * n2 + j) * rows, 16), rows), :]

    def send(source, target, s, r, where):
        copy = pltpu.make_async_remote_copy(
            src_ref=source, dst_ref=target, send_sem=s, recv_sem=r,
            device_id=where, device_id_type=MESH,
        )
        copy.start()
        started.append(copy)
        return copy

    def other(k):
        return lax.rem(x + k, n1)

    def along(j):
        return lax.rem(y + j, n2)

    order = list(range(1, n2)) + [0]
    first, second, third, fourth = {}, {}, {}, {}
    held = []

    def scatter():
        for j in order:
            for k in range(1, n1):
                first[j, k] = send(
                    chunk(grads, other(k), along(j)), rx1.at[j, k], s1.at[j, k], r1.at[j, k],
                    {outer_name: other(k)},
                )

    def forward(j):
        for k in range(1, n1):
            first[j, k].wait_recv()
        summed = load(grads, x, along(j)).astype(f32)
        for k in range(1, n1):
            summed = summed + rx1[j, k].astype(f32)
        part[j] = summed.astype(bf16) if j else jnp.zeros(part.shape[1:], bf16)
        if j:
            second[j] = send(
                part.at[j], rx2.at[j], s2.at[j], r2.at[j], {inner_name: along(j)}
            )
        else:
            held.append(summed)

    def spread_out(j, scene):
        for k in range(1, n1):
            fourth[j, k] = send(
                chunk(out, x, scene), chunk(out, x, scene), s4.at[j, k], r4.at[j, k],
                {outer_name: other(k)},
            )

    def finish():
        summed = held[0]
        for j in range(1, n2):
            second[j].wait_recv()
            summed = summed + rx2[j].astype(f32)
        out[pl.ds(pl.multiple_of(base + (x * n2 + y) * rows, 16), rows), :] = summed.astype(bf16)
        for j in range(1, n2):
            third[j] = send(
                chunk(out, x, y), chunk(out, x, y), s3.at[j], r3.at[j], {inner_name: along(j)}
            )
        spread_out(0, y)

    def gather(j):
        third[j].wait_recv()
        spread_out(j, lax.rem(y + n2 - j, n2))

    def end():
        for copy in fourth.values():
            copy.wait_recv()

    return scatter, forward, finish, gather, end, order


def shifted(t, inside, side):
    if t == 0:
        return inside
    axis = inside.ndim - 2
    place = lax.broadcasted_iota(jnp.int32, inside.shape, axis)
    joined = jnp.where(place == (0 if t > 0 else 7), side, inside)
    return pltpu.roll(joined, 7 if t > 0 else 1, axis)


def whole_kernel(
    owners, scenes, cap, cuts, nb, route, feats, weights, projection, cotangent,
    acts, out,
    before, after, routes, routes_s, links, tables, full, plus, minus, ext, wide, taps, tiles, slots,
    z, slope, skip, factor, lifted, arrived, back, spread, grads, handed, landing, s_up, r_up, s_dn, r_dn, s_rt, r_rt, rs_sem,
    s_sem, r_sem, s_bk, r_bk, *rest,
):
    me = lax.axis_index("brick")
    scene = lax.axis_index("dp")
    section = lax.axis_index("section")
    bricks = feats.shape[0]
    barrier = pltpu.get_barrier_semaphore()
    for d in range(owners):
        pl.semaphore_signal(
            barrier, inc=1, device_id={"brick": d, "section": 1 - section}, device_id_type=MESH
        )
    for k in range(1, owners):
        pl.semaphore_signal(
            barrier, inc=1, device_id={"brick": lax.rem(me + k, owners)}, device_id_type=MESH
        )
    for k in range(1, scenes):
        pl.semaphore_signal(
            barrier, inc=1, device_id={"dp": lax.rem(scene + k, scenes)}, device_id_type=MESH
        )
    routes[me] = route[...]
    start = me * bricks

    def inside(index, last):
        return jnp.minimum(jnp.maximum(index, 0), last)

    for r in range(bricks):
        up = nb[r, 0]
        dn = nb[r, 1]
        links[r, 0] = inside(jnp.where(up >= 0, up - start, 2 * bricks), 2 * bricks)
        back_row = jnp.where(dn >= start, dn - start, dn - start + 2 * bricks)
        links[r, 1] = inside(jnp.where(dn >= 0, back_row, 2 * bricks), 2 * bricks)
        for e in range(2, 6):
            links[r, e] = inside(jnp.where(nb[r, e] >= 0, nb[r, e] - start, bricks), bricks)
    for e in range(6):
        links[bricks, e] = jnp.int32(2 * bricks if e < 2 else bricks)
    full[:bricks] = feats[...].astype(f32)
    full[bricks] = jnp.zeros(full.shape[1:], f32)
    for p in range(3):
        wide[:, p * 128 : (p + 1) * 128] = weights[9 * p : 9 * p + 9].reshape(1152, 128)
    pl.semaphore_wait(barrier, 2 * owners - 1 + scenes - 1)

    halo = [
        pltpu.make_async_remote_copy(
            src_ref=feats.at[:, 7], dst_ref=before, send_sem=s_up, recv_sem=r_up,
            device_id={"brick": lax.rem(me + 1, owners)}, device_id_type=MESH,
        ),
        pltpu.make_async_remote_copy(
            src_ref=feats.at[:, 0], dst_ref=after, send_sem=s_dn, recv_sem=r_dn,
            device_id={"brick": lax.rem(me + owners - 1, owners)}, device_id_type=MESH,
        ),
    ]
    for k in range(1, owners):
        halo.append(
            pltpu.make_async_remote_copy(
                src_ref=route, dst_ref=routes.at[me], send_sem=s_rt.at[k], recv_sem=r_rt.at[k],
                device_id={"brick": lax.rem(me + k, owners)}, device_id_type=MESH,
            )
        )
    for copy in halo:
        copy.start()

    def chains(r):
        r1 = {0: r, 1: links[r, 4], -1: links[r, 5]}
        r2 = {}
        for t in (-1, 0, 1):
            r2[0, t] = r1[t]
            r2[1, t] = links[r1[t], 2]
            r2[-1, t] = links[r1[t], 3]
        return r1, r2

    def inner_planes(r, carry):
        r1, r2 = chains(r)
        for t in (-1, 0, 1):
            ext[t + 1, 1:9, 1:9] = shifted(t, full[r], full[r1[t]])
            ext[t + 1, 1:9, 0] = shifted(t, full[r2[-1, 0], :, 7], full[r2[-1, t], :, 7])
            ext[t + 1, 1:9, 9] = shifted(t, full[r2[1, 0], :, 0], full[r2[1, t], :, 0])
        for q in range(3):
            for t in range(3):
                lane = (3 * q + t) * 128
                z[r, 64:576, lane : lane + 128] = (
                    ext[t, 1:9, q : q + 8].reshape(512, 128).astype(bf16)
                )
        return carry

    lax.fori_loop(0, bricks, inner_planes, 0)
    plus[:bricks] = feats[:, 0].astype(f32)
    plus[2 * bricks] = jnp.zeros(plus.shape[1:], f32)
    minus[:bricks] = feats[:, 7].astype(f32)
    minus[2 * bricks] = jnp.zeros(minus.shape[1:], f32)
    for copy in halo:
        copy.wait_recv()
    route_copy = pltpu.make_async_copy(routes, routes_s, rs_sem)
    route_copy.start()
    plus[bricks : 2 * bricks] = after[...].astype(f32)
    minus[bricks : 2 * bricks] = before[...].astype(f32)

    def outer_planes(r, carry):
        r1, r2 = chains(r)
        for p, table in ((-1, minus), (1, plus)):
            a = 0 if p < 0 else 9
            r3 = {place: links[r2[place], 0 if p > 0 else 1] for place in r2}
            for t in (-1, 0, 1):
                ext[t + 1, a, 1:9] = shifted(t, table[r3[0, 0]], table[r3[0, t]])
                ext[t + 1, a, 0] = shifted(t, table[r3[-1, 0], 7], table[r3[-1, t], 7])
                ext[t + 1, a, 9] = shifted(t, table[r3[1, 0], 0], table[r3[1, t], 0])
            for q in range(3):
                for t in range(3):
                    lane = (3 * q + t) * 128
                    z[r, 64 * a : 64 * a + 64, lane : lane + 128] = (
                        ext[t, a, q : q + 8].reshape(64, 128).astype(bf16)
                    )
        product = jnp.dot(z[r], wide[...], preferred_element_type=f32)
        total_taps = product[0:512, 0:128] + product[64:576, 128:256] + product[128:640, 256:384]
        taps[r] = total_taps
        tiles[r] = (total_taps / (1.0 + jnp.exp(-total_taps))).astype(bf16)
        return carry

    lax.fori_loop(0, bricks, outer_planes, 0)
    route_copy.wait()

    def places(s):
        targets = [inside(lax.div(routes_s[s, 0, r], bricks), owners - 1) for r in range(bricks)]
        counts = []
        for r in range(bricks):
            count = jnp.int32(0)
            for e in range(r):
                count = count + jnp.where(targets[e] == targets[r], 1, 0)
            counts.append(jnp.minimum(count, cap - 1))
        return targets, counts

    targets, counts = places(me)
    mine = [targets[r] * cap + counts[r] for r in range(bricks)]
    for r in range(bricks):
        tables[0, r] = mine[r]
    for i in range(owners * cap):
        which = jnp.int32(0)
        for r in range(1, bricks):
            which = jnp.where(mine[r] == i, r, which)
        tables[3, i] = which

    def one_owner(s, found):
        targets, counts = places(s)
        found = list(found)
        rows = [inside(lax.rem(routes_s[s, 0, r], bricks), bricks - 1) for r in range(bricks)]
        for r in range(bricks):
            for row in range(bricks):
                hit = jnp.logical_and(targets[r] == me, rows[r] == row)
                found[row] = jnp.where(hit, s * cap + counts[r], found[row])
        for j in range(cap):
            tag = jnp.int32(0)
            for r in range(bricks):
                hit = jnp.logical_and(targets[r] == me, counts[r] == j)
                tag = jnp.where(hit, rows[r], tag)
            tables[2, s * cap + j] = tag
        return tuple(found)

    found = lax.fori_loop(0, owners, one_owner, (jnp.int32(0),) * bricks)
    for row in range(bricks):
        tables[1, row] = found[row]

    pieces = s_sem.shape[0]
    height = 512 // pieces

    def move(c, k, source, sends, receives):
        peer = lax.rem(me + k, owners)
        return pltpu.make_async_remote_copy(
            src_ref=source.at[pl.ds(peer * cap, cap), pl.ds(c * height, height)],
            dst_ref=arrived[c].at[pl.ds(me * cap, cap)],
            send_sem=sends.at[c, k], recv_sem=receives.at[c, k],
            device_id={"brick": peer, "section": 1 - section}, device_id_type=MESH,
        )

    order = [k for k in range(1, owners)] + [0]

    @pl.when(section == 0)
    def _():
        for c in range(pieces):
            span = slice(c * height, (c + 1) * height)

            def fill(i, carry):
                slots[i, span] = tiles[tables[3, i], span]
                return carry

            lax.fori_loop(0, owners * cap, fill, 0)
            for k in order:
                move(c, k, slots, s_sem, r_sem).start()
        skip[...] = jnp.zeros(skip.shape, skip.dtype)

        def gate(r, carry):
            v = taps[r]
            g = 1.0 / (1.0 + jnp.exp(-v))
            acts[r] = (v * g).astype(bf16)
            factor[r] = g * (1.0 + v * (1.0 - g))
            return carry

        lax.fori_loop(0, bricks, gate, 0)
        for c in range(pieces):
            for k in order:
                move(c, k, back, s_bk, r_bk).wait_recv()
            span = slice(c * height, (c + 1) * height)

            def last(r, carry):
                both = cotangent[r, span].astype(f32) + arrived[c][tables[0, r]].astype(f32)
                slope[r, span] = (both * factor[r, span]).astype(bf16)
                return carry

            lax.fori_loop(0, bricks, last, 0)

    @pl.when(section == 1)
    def _():
        for c in range(pieces):
            for k in order:
                move(c, k, slots, s_sem, r_sem).wait_recv()
            span = slice(c * height, (c + 1) * height)

            def step(r, carry):
                tile = arrived[c][tables[1, r]]
                skip[r, span] = tile
                v = taps[r, span] + jnp.dot(tile, projection[...], preferred_element_type=f32)
                g = 1.0 / (1.0 + jnp.exp(-v))
                acts[r, span] = (v * g).astype(bf16)
                down = (cotangent[r, span].astype(f32) * (g * (1.0 + v * (1.0 - g)))).astype(bf16)
                slope[r, span] = down
                lifted[r, span] = lax.dot_general(
                    down, projection[...], (((1,), (1,)), ((), ())), preferred_element_type=f32
                ).astype(bf16)
                return carry

            lax.fori_loop(0, bricks, step, 0)

            def pack(i, carry):
                back[i, span] = lifted[tables[2, i], span]
                return carry

            lax.fori_loop(0, owners * cap, pack, 0)
            for k in order:
                move(c, k, back, s_bk, r_bk).start()

    spread[...] = jnp.zeros(spread.shape, bf16)
    for p in range(3):
        spread[:, p * 64 : p * 64 + 512, p * 128 : (p + 1) * 128] = slope[...]
    hand = pltpu.make_async_remote_copy(
        src_ref=grads.at[pl.ds(3456, 128)], dst_ref=handed, send_sem=rest[0], recv_sem=rest[1],
        device_id={"section": 1 - section}, device_id_type=MESH,
    )

    @pl.when(section == 1)
    def _():
        grads[3456:3584] = lax.dot_general(
            skip[...].reshape(bricks * 512, 128), slope[...].reshape(bricks * 512, 128),
            (((0,), (0,)), ((), ())), preferred_element_type=f32,
        ).astype(bf16)
        hand.start()

    if grads.shape[0] > 3584:
        grads[3584:] = jnp.zeros((grads.shape[0] - 3584, 128), bf16)

    started = []
    on_brick, on_dp = ("brick", owners), ("dp", scenes)
    parts = []
    for i in range(3):
        outer, inner = (on_dp, on_brick) if i == 0 else (on_brick, on_dp)
        parts.append(
            reduce_part(
                grads, out, cuts[i], outer, inner, *landing[i],
                rest[2 + 8 * i : 10 + 8 * i], started,
            )
        )
    for q in range(3):
        product = lax.dot_general(
            z[:, :, 384 * q : 384 * (q + 1)].reshape(bricks * 640, 384),
            spread[...].reshape(bricks * 640, 384),
            (((0,), (0,)), ((), ())), preferred_element_type=f32,
        )
        for p in range(3):
            first_row = 384 * (3 * q + p)
            grads[first_row : first_row + 384] = product[:, p * 128 : (p + 1) * 128].astype(bf16)
        if q == 2:

            @pl.when(section == 0)
            def _():
                hand.wait_recv()
                grads[3456:3584] = handed[...]

        parts[q][0]()
    for i in range(max(owners, scenes)):
        for way in parts:
            if i < len(way[5]):
                way[1](way[5][i])
    for way in parts:
        way[2]()
    for i in range(1, max(owners, scenes)):
        for way in parts:
            if i < len(way[5]):
                way[3](i)
    for way in parts:
        way[4]()

    @pl.when(section == 1)
    def _():
        hand.wait_send()
        for c in range(pieces):
            for k in order:
                move(c, k, back, s_bk, r_bk).wait_send()

    @pl.when(section == 0)
    def _():
        for c in range(pieces):
            for k in order:
                move(c, k, slots, s_sem, r_sem).wait_send()

    for copy in started:
        copy.wait_send()
    for copy in halo:
        copy.wait_send()


def tail_kernel(
    summed, acts, weight_out, proj_out, acts_out,
    narrow, wider, held, in_sem, out_sem, a_in, a_out,
):
    rows = 384
    hold = pltpu.make_async_copy(acts, held, a_in)
    keep = pltpu.make_async_copy(held, acts_out, a_out)
    fetch, store = [], []
    for q in range(3):
        size = 1152 if q < 2 else 1280
        span = pl.ds(1152 * q, size)
        fetch.append(pltpu.make_async_copy(summed.at[span], narrow.at[span], in_sem.at[q]))
        fetch[q].start()
    hold.start()
    for q in range(3):
        fetch[q].wait()
        for p in range(3):
            place = rows * (3 * q + p)
            wider[place : place + rows] = narrow[place : place + rows].astype(f32)
            copy = pltpu.make_async_copy(
                wider.at[pl.ds(place, rows)], weight_out.at[pl.ds(rows * (3 * p + q), rows)],
                out_sem.at[3 * q + p],
            )
            copy.start()
            store.append(copy)
    wider[3456:3584] = narrow[3456:3584].astype(f32)
    copy = pltpu.make_async_copy(wider.at[pl.ds(3456, 128)], proj_out, out_sem.at[9])
    copy.start()
    store.append(copy)
    hold.wait()
    keep.start()
    for copy in store:
        copy.wait()
    keep.wait()


def body(features, weights, projection, cotangent, neighbours, route):
    bricks, channels = features.shape[2], features.shape[-1]
    owners, scenes = lax.axis_size("brick"), lax.axis_size("dp")
    cap = max(2, 3 * bricks // (2 * owners))
    count = owners * cap
    feats = features[0, 0].reshape(bricks, 8, 8, 8, channels)
    dma, arr, vm = pltpu.SemaphoreType.DMA, jax.ShapeDtypeStruct, pltpu.VMEM
    plane = (bricks, 8, 8, channels)
    tile = (bricks, 512, channels)
    unit = 16 * owners * scenes
    units = -(-28 * channels // unit)
    total = units * unit
    cuts = [0, 9 * channels // unit * unit, 18 * channels // unit * unit, total]
    heights = [(cuts[i + 1] - cuts[i]) // (owners * scenes) for i in range(3)]
    landing, signals = [], []
    for i in range(3):
        n1, n2 = (scenes, owners) if i == 0 else (owners, scenes)
        landing.append(
            [
                vm((n2, n1, heights[i], channels), bf16),
                vm((n2, heights[i], channels), bf16),
                vm((n2, heights[i], channels), bf16),
            ]
        )
        signals += [dma((n2, n1))] * 2 + [dma((n2,))] * 4 + [dma((n2, n1))] * 2
    pieces = 4
    anywhere = pl.BlockSpec(memory_space=pl.ANY)
    acts, summed = pl.pallas_call(
        functools.partial(whole_kernel, owners, scenes, cap, cuts),
        out_shape=[arr(tile, bf16), arr((total, channels), bf16)],
        in_specs=[SM, VM, VM, VM, VM, VM],
        out_specs=[VM, VM],
        scratch_shapes=[
            vm(plane, bf16), vm(plane, bf16), vm((owners, 1, bricks), jnp.int32),
            pltpu.SMEM((owners, 1, bricks), jnp.int32), pltpu.SMEM((bricks + 1, 6), jnp.int32),
            pltpu.SMEM((4, max(count, bricks)), jnp.int32),
            vm((bricks + 1, 8, 8, 8, channels), f32),
            vm((2 * bricks + 1, 8, 8, channels), f32),
            vm((2 * bricks + 1, 8, 8, channels), f32),
            vm((3, 10, 10, 8, channels), f32),
            vm((9 * channels, 3 * channels), bf16),
            vm(tile, f32), vm(tile, bf16), vm((count, 512, channels), bf16),
            vm((bricks, 640, 9 * channels), bf16),
            vm(tile, bf16), vm(tile, bf16), vm(tile, f32), vm(tile, bf16),
            [vm((count, 512 // pieces, channels), bf16) for _ in range(pieces)],
            vm((count, 512, channels), bf16),
            vm((bricks, 640, 3 * channels), bf16),
            vm((total, channels), bf16), vm((channels, channels), bf16), landing,
            dma, dma, dma, dma, dma((owners,)), dma((owners,)), dma,
            *[dma((pieces, owners)) for _ in range(4)],
            dma, dma, *signals,
        ],
        compiler_params=params(0),
    )(neighbours[0, 0], route, feats, weights[0], projection, cotangent[0, 0])

    weight_sum, projection_sum, acts = pl.pallas_call(
        tail_kernel,
        out_shape=[
            arr((27 * channels, channels), f32), arr((channels, channels), f32), arr(tile, bf16)
        ],
        in_specs=[anywhere] * 2,
        out_specs=[anywhere] * 3,
        scratch_shapes=[
            vm((28 * channels, channels), bf16), vm((28 * channels, channels), f32),
            vm(tile, bf16), dma((3,)), dma((10,)), dma, dma,
        ],
        compiler_params=params(),
    )(summed, acts)
    return (
        acts[None, None],
        weight_sum.reshape(1, 27, channels, channels),
        projection_sum,
    )


def solution(mesh):
    return jax.shard_map(
        body,
        mesh=mesh,
        in_specs=(
            P("section", "dp", "brick", None, None),
            P("section", None, None, None),
            P(),
            P("section", "dp", "brick", None, None),
            P("section", "dp", "brick", None),
            P("dp", "brick"),
        ),
        out_specs=(P("section", "dp", "brick", None, None), P("section", None, None, None), P()),
        check_vma=False,
    )
```

```python
import functools

import jax
import jax.numpy as jnp
from jax import lax
from jax.experimental import pallas as pl
from jax.experimental.pallas import tpu as pltpu
from jax.sharding import PartitionSpec as P

MESH = pl.DeviceIdType.MESH
f32, bf16 = jnp.float32, jnp.bfloat16
VM = pl.BlockSpec(memory_space=pltpu.VMEM)
SM = pl.BlockSpec(memory_space=pltpu.SMEM)
LIMIT = 56 * 1024 * 1024


def params(collective=None):
    if collective is None:
        return pltpu.CompilerParams(vmem_limit_bytes=LIMIT)
    return pltpu.CompilerParams(
        vmem_limit_bytes=LIMIT, collective_id=collective, has_side_effects=True
    )


def reduce_part(grads, out, base, outer, inner, rx1, part, rx2, sems, started):
    (outer_name, n1), (inner_name, n2) = outer, inner
    x, y = lax.axis_index(outer_name), lax.axis_index(inner_name)
    rows = rx2.shape[1]
    s1, r1, s2, r2, s3, r3, s4, r4 = sems

    def chunk(ref, i, j):
        return ref.at[pl.ds(pl.multiple_of(base + (i * n2 + j) * rows, 16), rows)]

    def load(ref, i, j):
        return ref[pl.ds(pl.multiple_of(base + (i * n2 + j) * rows, 16), rows), :]

    def send(source, target, s, r, where):
        copy = pltpu.make_async_remote_copy(
            src_ref=source, dst_ref=target, send_sem=s, recv_sem=r,
            device_id=where, device_id_type=MESH,
        )
        copy.start()
        started.append(copy)
        return copy

    def other(k):
        return lax.rem(x + k, n1)

    def along(j):
        return lax.rem(y + j, n2)

    order = list(range(1, n2)) + [0]
    first, second, third, fourth = {}, {}, {}, {}
    held = []

    def scatter():
        for j in order:
            for k in range(1, n1):
                first[j, k] = send(
                    chunk(grads, other(k), along(j)), rx1.at[j, k], s1.at[j, k], r1.at[j, k],
                    {outer_name: other(k)},
                )

    def forward(j):
        for k in range(1, n1):
            first[j, k].wait_recv()
        summed = load(grads, x, along(j)).astype(f32)
        for k in range(1, n1):
            summed = summed + rx1[j, k].astype(f32)
        part[j] = summed.astype(bf16) if j else jnp.zeros(part.shape[1:], bf16)
        if j:
            second[j] = send(
                part.at[j], rx2.at[j], s2.at[j], r2.at[j], {inner_name: along(j)}
            )
        else:
            held.append(summed)

    def spread_out(j, scene):
        for k in range(1, n1):
            fourth[j, k] = send(
                chunk(out, x, scene), chunk(out, x, scene), s4.at[j, k], r4.at[j, k],
                {outer_name: other(k)},
            )

    def finish():
        summed = held[0]
        for j in range(1, n2):
            second[j].wait_recv()
            summed = summed + rx2[j].astype(f32)
        out[pl.ds(pl.multiple_of(base + (x * n2 + y) * rows, 16), rows), :] = summed.astype(bf16)
        for j in range(1, n2):
            third[j] = send(
                chunk(out, x, y), chunk(out, x, y), s3.at[j], r3.at[j], {inner_name: along(j)}
            )
        spread_out(0, y)

    def gather(j):
        third[j].wait_recv()
        spread_out(j, lax.rem(y + n2 - j, n2))

    def end():
        for copy in fourth.values():
            copy.wait_recv()

    return scatter, forward, finish, gather, end, order


def shifted(t, inside, side):
    if t == 0:
        return inside
    axis = inside.ndim - 2
    place = lax.broadcasted_iota(jnp.int32, inside.shape, axis)
    joined = jnp.where(place == (0 if t > 0 else 7), side, inside)
    return pltpu.roll(joined, 7 if t > 0 else 1, axis)


def whole_kernel(
    owners, scenes, cap, cuts, nb, route, feats, weights, projection, cotangent,
    acts, out,
    before, after, routes, routes_s, links, tables, full, plus, minus, ext, wide, taps, tiles, slots,
    z, slope, skip, factor, lifted, arrived, back, spread, grads, handed, landing, s_up, r_up, s_dn, r_dn, s_rt, r_rt, rs_sem,
    s_sem, r_sem, s_bk, r_bk, *rest,
):
    me = lax.axis_index("brick")
    scene = lax.axis_index("dp")
    section = lax.axis_index("section")
    bricks = feats.shape[0]
    barrier = pltpu.get_barrier_semaphore()
    for d in range(owners):
        pl.semaphore_signal(
            barrier, inc=1, device_id={"brick": d, "section": 1 - section}, device_id_type=MESH
        )
    for k in range(1, owners):
        pl.semaphore_signal(
            barrier, inc=1, device_id={"brick": lax.rem(me + k, owners)}, device_id_type=MESH
        )
    for k in range(1, scenes):
        pl.semaphore_signal(
            barrier, inc=1, device_id={"dp": lax.rem(scene + k, scenes)}, device_id_type=MESH
        )
    routes[me] = route[...]
    start = me * bricks

    def inside(index, last):
        return jnp.minimum(jnp.maximum(index, 0), last)

    for r in range(bricks):
        up = nb[r, 0]
        dn = nb[r, 1]
        links[r, 0] = inside(jnp.where(up >= 0, up - start, 2 * bricks), 2 * bricks)
        back_row = jnp.where(dn >= start, dn - start, dn - start + 2 * bricks)
        links[r, 1] = inside(jnp.where(dn >= 0, back_row, 2 * bricks), 2 * bricks)
        for e in range(2, 6):
            links[r, e] = inside(jnp.where(nb[r, e] >= 0, nb[r, e] - start, bricks), bricks)
    for e in range(6):
        links[bricks, e] = jnp.int32(2 * bricks if e < 2 else bricks)
    full[:bricks] = feats[...].astype(f32)
    full[bricks] = jnp.zeros(full.shape[1:], f32)
    for p in range(3):
        wide[:, p * 128 : (p + 1) * 128] = weights[9 * p : 9 * p + 9].reshape(1152, 128)
    pl.semaphore_wait(barrier, 2 * owners - 1 + scenes - 1)

    halo = [
        pltpu.make_async_remote_copy(
            src_ref=feats.at[:, 7], dst_ref=before, send_sem=s_up, recv_sem=r_up,
            device_id={"brick": lax.rem(me + 1, owners)}, device_id_type=MESH,
        ),
        pltpu.make_async_remote_copy(
            src_ref=feats.at[:, 0], dst_ref=after, send_sem=s_dn, recv_sem=r_dn,
            device_id={"brick": lax.rem(me + owners - 1, owners)}, device_id_type=MESH,
        ),
    ]
    for k in range(1, owners):
        halo.append(
            pltpu.make_async_remote_copy(
                src_ref=route, dst_ref=routes.at[me], send_sem=s_rt.at[k], recv_sem=r_rt.at[k],
                device_id={"brick": lax.rem(me + k, owners)}, device_id_type=MESH,
            )
        )
    for copy in halo:
        copy.start()

    def chains(r):
        r1 = {0: r, 1: links[r, 4], -1: links[r, 5]}
        r2 = {}
        for t in (-1, 0, 1):
            r2[0, t] = r1[t]
            r2[1, t] = links[r1[t], 2]
            r2[-1, t] = links[r1[t], 3]
        return r1, r2

    def inner_planes(r, carry):
        r1, r2 = chains(r)
        for t in (-1, 0, 1):
            ext[t + 1, 1:9, 1:9] = shifted(t, full[r], full[r1[t]])
            ext[t + 1, 1:9, 0] = shifted(t, full[r2[-1, 0], :, 7], full[r2[-1, t], :, 7])
            ext[t + 1, 1:9, 9] = shifted(t, full[r2[1, 0], :, 0], full[r2[1, t], :, 0])
        for q in range(3):
            for t in range(3):
                lane = (3 * q + t) * 128
                z[r, 64:576, lane : lane + 128] = (
                    ext[t, 1:9, q : q + 8].reshape(512, 128).astype(bf16)
                )
        return carry

    lax.fori_loop(0, bricks, inner_planes, 0)
    plus[:bricks] = feats[:, 0].astype(f32)
    plus[2 * bricks] = jnp.zeros(plus.shape[1:], f32)
    minus[:bricks] = feats[:, 7].astype(f32)
    minus[2 * bricks] = jnp.zeros(minus.shape[1:], f32)
    for copy in halo:
        copy.wait_recv()
    route_copy = pltpu.make_async_copy(routes, routes_s, rs_sem)
    route_copy.start()
    plus[bricks : 2 * bricks] = after[...].astype(f32)
    minus[bricks : 2 * bricks] = before[...].astype(f32)

    def outer_planes(r, carry):
        r1, r2 = chains(r)
        for p, table in ((-1, minus), (1, plus)):
            a = 0 if p < 0 else 9
            r3 = {place: links[r2[place], 0 if p > 0 else 1] for place in r2}
            for t in (-1, 0, 1):
                ext[t + 1, a, 1:9] = shifted(t, table[r3[0, 0]], table[r3[0, t]])
                ext[t + 1, a, 0] = shifted(t, table[r3[-1, 0], 7], table[r3[-1, t], 7])
                ext[t + 1, a, 9] = shifted(t, table[r3[1, 0], 0], table[r3[1, t], 0])
            for q in range(3):
                for t in range(3):
                    lane = (3 * q + t) * 128
                    z[r, 64 * a : 64 * a + 64, lane : lane + 128] = (
                        ext[t, a, q : q + 8].reshape(64, 128).astype(bf16)
                    )
        return carry

    lax.fori_loop(0, bricks, outer_planes, 0)
    route_copy.wait()

    def places(s):
        targets = [inside(lax.div(routes_s[s, 0, r], bricks), owners - 1) for r in range(bricks)]
        counts = []
        for r in range(bricks):
            count = jnp.int32(0)
            for e in range(r):
                count = count + jnp.where(targets[e] == targets[r], 1, 0)
            counts.append(jnp.minimum(count, cap - 1))
        return targets, counts

    targets, counts = places(me)
    mine = [targets[r] * cap + counts[r] for r in range(bricks)]
    for r in range(bricks):
        tables[0, r] = mine[r]
    for i in range(owners * cap):
        which = jnp.int32(0)
        for r in range(1, bricks):
            which = jnp.where(mine[r] == i, r, which)
        tables[3, i] = which

    def one_owner(s, found):
        targets, counts = places(s)
        found = list(found)
        rows = [inside(lax.rem(routes_s[s, 0, r], bricks), bricks - 1) for r in range(bricks)]
        for r in range(bricks):
            for row in range(bricks):
                hit = jnp.logical_and(targets[r] == me, rows[r] == row)
                found[row] = jnp.where(hit, s * cap + counts[r], found[row])
        for j in range(cap):
            tag = jnp.int32(0)
            for r in range(bricks):
                hit = jnp.logical_and(targets[r] == me, counts[r] == j)
                tag = jnp.where(hit, rows[r], tag)
            tables[2, s * cap + j] = tag
        return tuple(found)

    found = lax.fori_loop(0, owners, one_owner, (jnp.int32(0),) * bricks)
    for row in range(bricks):
        tables[1, row] = found[row]


    pieces = s_sem.shape[0]
    height = 512 // pieces

    def move(c, k, source, sends, receives):
        peer = lax.rem(me + k, owners)
        return pltpu.make_async_remote_copy(
            src_ref=source.at[pl.ds(peer * cap, cap), pl.ds(c * height, height)],
            dst_ref=arrived[c].at[pl.ds(me * cap, cap)],
            send_sem=sends.at[c, k], recv_sem=receives.at[c, k],
            device_id={"brick": peer, "section": 1 - section}, device_id_type=MESH,
        )

    order = [k for k in range(1, owners)] + [0]
    for c in range(pieces):
        span = slice(c * height, (c + 1) * height)
        chunk_taps = jnp.zeros((bricks * height, 128), f32)
        for p in range(3):
            low = c * height + 64 * p
            chunk_taps = chunk_taps + jnp.dot(
                z[:, low : low + height].reshape(bricks * height, 1152),
                wide[:, p * 128 : (p + 1) * 128],
                preferred_element_type=f32,
            )
        taps[:, span] = chunk_taps.reshape(bricks, height, 128)

        @pl.when(section == 0)
        def _():
            v = taps[:, span]
            tiles[:, span] = (v / (1.0 + jnp.exp(-v))).astype(bf16)

            def fill(i, carry):
                slots[i, span] = tiles[tables[3, i], span]
                return carry

            lax.fori_loop(0, owners * cap, fill, 0)
            for k in order:
                move(c, k, slots, s_sem, r_sem).start()

    @pl.when(section == 0)
    def _():

        def gate(r, carry):
            v = taps[r]
            g = 1.0 / (1.0 + jnp.exp(-v))
            acts[r] = (v * g).astype(bf16)
            factor[r] = g * (1.0 + v * (1.0 - g))
            return carry

        lax.fori_loop(0, bricks, gate, 0)
        for c in range(pieces):
            for k in order:
                move(c, k, back, s_bk, r_bk).wait_recv()
            span = slice(c * height, (c + 1) * height)

            def last(r, carry):
                both = cotangent[r, span].astype(f32) + arrived[c][tables[0, r]].astype(f32)
                slope[r, span] = (both * factor[r, span]).astype(bf16)
                return carry

            lax.fori_loop(0, bricks, last, 0)

    @pl.when(section == 1)
    def _():
        for c in range(pieces):
            for k in order:
                move(c, k, slots, s_sem, r_sem).wait_recv()
            span = slice(c * height, (c + 1) * height)

            def step(r, carry):
                tile = arrived[c][tables[1, r]]
                skip[r, span] = tile
                v = taps[r, span] + jnp.dot(tile, projection[...], preferred_element_type=f32)
                g = 1.0 / (1.0 + jnp.exp(-v))
                acts[r, span] = (v * g).astype(bf16)
                down = (cotangent[r, span].astype(f32) * (g * (1.0 + v * (1.0 - g)))).astype(bf16)
                slope[r, span] = down
                lifted[r, span] = lax.dot_general(
                    down, projection[...], (((1,), (1,)), ((), ())), preferred_element_type=f32
                ).astype(bf16)
                return carry

            lax.fori_loop(0, bricks, step, 0)

            def pack(i, carry):
                back[i, span] = lifted[tables[2, i], span]
                return carry

            lax.fori_loop(0, owners * cap, pack, 0)
            for k in order:
                move(c, k, back, s_bk, r_bk).start()

    spread[...] = jnp.zeros(spread.shape, bf16)
    for p in range(3):
        spread[:, p * 64 : p * 64 + 512, p * 128 : (p + 1) * 128] = slope[...]
    hand = pltpu.make_async_remote_copy(
        src_ref=grads.at[pl.ds(3456, 128)], dst_ref=handed, send_sem=rest[0], recv_sem=rest[1],
        device_id={"section": 1 - section}, device_id_type=MESH,
    )

    @pl.when(section == 1)
    def _():
        grads[3456:3584] = lax.dot_general(
            skip[...].reshape(bricks * 512, 128), slope[...].reshape(bricks * 512, 128),
            (((0,), (0,)), ((), ())), preferred_element_type=f32,
        ).astype(bf16)
        hand.start()

    if grads.shape[0] > 3584:
        grads[3584:] = jnp.zeros((grads.shape[0] - 3584, 128), bf16)

    started = []
    on_brick, on_dp = ("brick", owners), ("dp", scenes)
    parts = []
    for i in range(3):
        outer, inner = (on_dp, on_brick) if i == 0 else (on_brick, on_dp)
        parts.append(
            reduce_part(
                grads, out, cuts[i], outer, inner, *landing[i],
                rest[2 + 8 * i : 10 + 8 * i], started,
            )
        )
    for q in range(3):
        product = lax.dot_general(
            z[:, :, 384 * q : 384 * (q + 1)].reshape(bricks * 640, 384),
            spread[...].reshape(bricks * 640, 384),
            (((0,), (0,)), ((), ())), preferred_element_type=f32,
        )
        for p in range(3):
            first_row = 384 * (3 * q + p)
            grads[first_row : first_row + 384] = product[:, p * 128 : (p + 1) * 128].astype(bf16)
        if q == 2:

            @pl.when(section == 0)
            def _():
                hand.wait_recv()
                grads[3456:3584] = handed[...]

        parts[q][0]()
    for i in range(max(owners, scenes)):
        for way in parts:
            if i < len(way[5]):
                way[1](way[5][i])
    for way in parts:
        way[2]()
    for i in range(1, max(owners, scenes)):
        for way in parts:
            if i < len(way[5]):
                way[3](i)
    for way in parts:
        way[4]()

    @pl.when(section == 1)
    def _():
        hand.wait_send()
        for c in range(pieces):
            for k in order:
                move(c, k, back, s_bk, r_bk).wait_send()

    @pl.when(section == 0)
    def _():
        for c in range(pieces):
            for k in order:
                move(c, k, slots, s_sem, r_sem).wait_send()

    for copy in started:
        copy.wait_send()
    for copy in halo:
        copy.wait_send()


def tail_kernel(
    summed, acts, weight_out, proj_out, acts_out,
    narrow, wider, held, in_sem, out_sem, a_in, a_out,
):
    rows = 384
    hold = pltpu.make_async_copy(acts, held, a_in)
    keep = pltpu.make_async_copy(held, acts_out, a_out)
    fetch, store = [], []
    for q in range(3):
        size = 1152 if q < 2 else 1280
        span = pl.ds(1152 * q, size)
        fetch.append(pltpu.make_async_copy(summed.at[span], narrow.at[span], in_sem.at[q]))
        fetch[q].start()
    hold.start()
    for q in range(3):
        fetch[q].wait()
        for p in range(3):
            place = rows * (3 * q + p)
            wider[place : place + rows] = narrow[place : place + rows].astype(f32)
            copy = pltpu.make_async_copy(
                wider.at[pl.ds(place, rows)], weight_out.at[pl.ds(rows * (3 * p + q), rows)],
                out_sem.at[3 * q + p],
            )
            copy.start()
            store.append(copy)
    wider[3456:3584] = narrow[3456:3584].astype(f32)
    copy = pltpu.make_async_copy(wider.at[pl.ds(3456, 128)], proj_out, out_sem.at[9])
    copy.start()
    store.append(copy)
    hold.wait()
    keep.start()
    for copy in store:
        copy.wait()
    keep.wait()


def body(features, weights, projection, cotangent, neighbours, route):
    bricks, channels = features.shape[2], features.shape[-1]
    owners, scenes = lax.axis_size("brick"), lax.axis_size("dp")
    cap = max(2, 3 * bricks // (2 * owners))
    count = owners * cap
    feats = features[0, 0].reshape(bricks, 8, 8, 8, channels)
    dma, arr, vm = pltpu.SemaphoreType.DMA, jax.ShapeDtypeStruct, pltpu.VMEM
    plane = (bricks, 8, 8, channels)
    tile = (bricks, 512, channels)
    unit = 16 * owners * scenes
    units = -(-28 * channels // unit)
    total = units * unit
    cuts = [0, 9 * channels // unit * unit, 18 * channels // unit * unit, total]
    heights = [(cuts[i + 1] - cuts[i]) // (owners * scenes) for i in range(3)]
    landing, signals = [], []
    for i in range(3):
        n1, n2 = (scenes, owners) if i == 0 else (owners, scenes)
        landing.append(
            [
                vm((n2, n1, heights[i], channels), bf16),
                vm((n2, heights[i], channels), bf16),
                vm((n2, heights[i], channels), bf16),
            ]
        )
        signals += [dma((n2, n1))] * 2 + [dma((n2,))] * 4 + [dma((n2, n1))] * 2
    pieces = 4
    anywhere = pl.BlockSpec(memory_space=pl.ANY)
    acts, summed = pl.pallas_call(
        functools.partial(whole_kernel, owners, scenes, cap, cuts),
        out_shape=[arr(tile, bf16), arr((total, channels), bf16)],
        in_specs=[SM, VM, VM, VM, VM, VM],
        out_specs=[VM, VM],
        scratch_shapes=[
            vm(plane, bf16), vm(plane, bf16), vm((owners, 1, bricks), jnp.int32),
            pltpu.SMEM((owners, 1, bricks), jnp.int32), pltpu.SMEM((bricks + 1, 6), jnp.int32),
            pltpu.SMEM((4, max(count, bricks)), jnp.int32),
            vm((bricks + 1, 8, 8, 8, channels), f32),
            vm((2 * bricks + 1, 8, 8, channels), f32),
            vm((2 * bricks + 1, 8, 8, channels), f32),
            vm((3, 10, 10, 8, channels), f32),
            vm((9 * channels, 3 * channels), bf16),
            vm(tile, f32), vm(tile, bf16), vm((count, 512, channels), bf16),
            vm((bricks, 640, 9 * channels), bf16),
            vm(tile, bf16), vm(tile, bf16), vm(tile, f32), vm(tile, bf16),
            [vm((count, 512 // pieces, channels), bf16) for _ in range(pieces)],
            vm((count, 512, channels), bf16),
            vm((bricks, 640, 3 * channels), bf16),
            vm((total, channels), bf16), vm((channels, channels), bf16), landing,
            dma, dma, dma, dma, dma((owners,)), dma((owners,)), dma,
            *[dma((pieces, owners)) for _ in range(4)],
            dma, dma, *signals,
        ],
        compiler_params=params(0),
    )(neighbours[0, 0], route, feats, weights[0], projection, cotangent[0, 0])

    weight_sum, projection_sum, acts = pl.pallas_call(
        tail_kernel,
        out_shape=[
            arr((27 * channels, channels), f32), arr((channels, channels), f32), arr(tile, bf16)
        ],
        in_specs=[anywhere] * 2,
        out_specs=[anywhere] * 3,
        scratch_shapes=[
            vm((28 * channels, channels), bf16), vm((28 * channels, channels), f32),
            vm(tile, bf16), dma((3,)), dma((10,)), dma, dma,
        ],
        compiler_params=params(),
    )(summed, acts)
    return (
        acts[None, None],
        weight_sum.reshape(1, 27, channels, channels),
        projection_sum,
    )


def solution(mesh):
    return jax.shard_map(
        body,
        mesh=mesh,
        in_specs=(
            P("section", "dp", "brick", None, None),
            P("section", None, None, None),
            P(),
            P("section", "dp", "brick", None, None),
            P("section", "dp", "brick", None),
            P("dp", "brick"),
        ),
        out_specs=(P("section", "dp", "brick", None, None), P("section", None, None, None), P()),
        check_vma=False,
    )
```
